32 devices in a mesh: grp: 2 (over x), layer: 16 (over z, y, core).
Axes of the slice: x: 2, y: 2, z: 4, core: 2. Of those that a mesh axis runs over, the one named last changes fastest.
Arguments:
- rhs: float32 [32, 16, 16, 128], P('layer', 'grp'), parts along dimension 1, may hold values from -6 to 6
- coeffs: float32 [32, 13, 16, 128], P('layer'), as said below
- transmit: float32 [32, 16, 128], P('layer'), as said below
- counts: int32 [16], replicated, may hold values from 1 to 2, as said below
- elec_x: int32 [16], P('grp'), parts along dimension 0, may hold values from 0 to 15
- elec_y: int32 [16], P('grp'), parts along dimension 0, may hold values from 0 to 127
Outputs:
- forward: float32 [32, 16, 16, 128], P('layer', 'grp'), parts along dimension 1
- backward: float32 [32, 16, 16, 128], P('layer', 'grp'), parts along dimension 1
The draws below stay inside these ranges and needn't reach their ends.
There are 2 independent parts, one for each index of `grp`. The reference program is written for one: setup_inputs(seed, part) draws one part's arguments, and reference() takes and returns one part's arrays. A program takes and returns all parts, laid end to end along the dimension named above; an argument that names none is the same for every part. Nothing has to cross between parts.
Inputs may be any that keep to these rules, and one draw needn't show every extreme that they name: Every index of layer uses its first counts entries of its 2 slots; some index uses all 2 and some only one. `coeffs`: centre coefficients lie in 1 to 2 and the twelve neighbour coefficients in 0.01 to 0.06. `transmit`: entries lie in 0 to 1.
All inputs are finite; a program needn't handle non-finite values.
Results may differ from the reference program's by a relative error of at most 0.0001.
Values sent between devices are 32-bit elements; how exact they have to be, the bound alone decides.
No kernel may reach another device: no remote copies, remote signals or barrier semaphores. Data moves between devices by JAX's collectives and lax.ppermute only.
A program may use at most 64 MiB of HBM per device.

```python
import math
import jax
import jax.numpy as jnp
from jax import lax

SRC = 8
PX = 16
PY = 128
CAP = 2
CHEB = 4
LAYER_SLOTS = 32


def draw_coeffs(key, part):
    first_key, second_key = jax.random.split(key, 2)
    center = jax.random.uniform(first_key, (LAYER_SLOTS, 1, PX, PY), jnp.float32, 1.0, 2.0)
    others = jax.random.uniform(second_key, (LAYER_SLOTS, 12, PX, PY), jnp.float32, 0.01, 0.06)
    return jnp.concatenate([center, others], axis=1)


def draw_transmit(key, part):
    random_key_list = jax.random.split(key, 4)
    lowest = math.log(0.3 / LAYER_SLOTS)
    highest = math.log(1.0 / 30.0)
    decay_rates = jnp.exp(jax.random.uniform(random_key_list[0], (PX, PY), jnp.float32, lowest, highest))
    random_shift = jax.random.uniform(random_key_list[1], (LAYER_SLOTS, PX, PY), jnp.float32, 0.5, 1.5)
    pulse_layer_group = jax.random.randint(random_key_list[2], (3,), 0, LAYER_SLOTS)
    layer_depth = jax.random.uniform(random_key_list[3], (3,), jnp.float32, 0.5, 0.8)
    contact_count = jnp.arange(LAYER_SLOTS)[:, None] == pulse_layer_group[None, :]
    pulse_groups = jnp.prod(jnp.where(contact_count, layer_depth[None, :], 1.0), axis=1)
    return jnp.exp(-decay_rates[None] * random_shift) * pulse_groups[:, None, None]


def draw_counts(key, part):
    random_key_list = jax.random.split(key, 3)
    number = LAYER_SLOTS // CAP
    base = jax.random.randint(random_key_list[0], (number,), 1, CAP + 1)
    fullest = jax.random.randint(random_key_list[1], (), 0, number)
    emptiest = (fullest + 1 + jax.random.randint(random_key_list[2], (), 0, number - 1)) % number
    places = jnp.arange(number)
    base = jnp.where(places == fullest, CAP, base)
    return jnp.where(places == emptiest, 1, base).astype(jnp.int32)


def plant(values, stream_key, least, largest):
    longest = values.shape.index(max(values.shape))
    spots = []
    for shift in (0, 1):
        where = [jax.random.randint(jax.random.fold_in(stream_key, axis), (), 0, length) for axis, length in enumerate(values.shape)]
        where[longest] = (where[longest] + shift) % values.shape[longest]
        spots.append(tuple(where))
    return values.at[spots[0]].set(least).at[spots[1]].set(largest)


def levels(stream_key, shape, pieces, low, high):
    loudness = 1.0
    for dim, blocks in pieces:
        steps = jax.random.uniform(jax.random.fold_in(jax.random.fold_in(stream_key, 6), dim), (blocks,), jnp.float32, low / len(pieces), high / len(pieces))
        loudness = loudness * jnp.repeat(jnp.exp(steps), shape[dim] // blocks).reshape((-1,) + (1,) * (len(shape) - 1 - dim))
    return loudness


def centred(key, shape, spread, most, shards=(), kind=jnp.bfloat16):
    values = spread * jax.random.normal(key, shape, jnp.float32)
    if shards:
        values = values * levels(key, shape, shards, -0.22, 0.18)
    return jnp.clip(values, -most, most).astype(kind)


def setup_inputs(seed: int = 0, part: int = 0) -> dict:
    splits = jax.random.split(jax.random.key(seed), 7)
    own_keys = jax.random.split(jax.random.fold_in(splits[6], part), 7)
    rhs = centred(own_keys[0], (LAYER_SLOTS, SRC, PX, PY), 1.0, 6.0, ((0, 16),), jnp.float32)
    coeffs = draw_coeffs(jax.random.fold_in(splits[6], 71), part)
    transmit = draw_transmit(jax.random.fold_in(splits[6], 71), part)
    counts = draw_counts(jax.random.fold_in(splits[6], 71), part)
    elec_x = plant(jax.random.randint(own_keys[4], (SRC,), 0, PX), jax.random.fold_in(own_keys[4], 1), 0, PX - 1).astype(jnp.int32)
    elec_y = plant(jax.random.randint(own_keys[5], (SRC,), 0, PY), jax.random.fold_in(own_keys[5], 1), 0, PY - 1).astype(jnp.int32)
    return {"rhs": rhs, "coeffs": coeffs, "transmit": transmit, "counts": counts, "elec_x": elec_x, "elec_y": elec_y}


STENCIL_OFFSETS = ((1, 0), (-1, 0), (0, 1), (0, -1), (2, 0), (-2, 0), (0, 2), (0, -2), (1, 1), (1, -1), (-1, 1), (-1, -1))
HALF_WIDTH = 0.72
INJECTED = 4.0


def plane_solve(source, plane_coeffs, passes):
    center = plane_coeffs[..., 0, :, :][..., None, :, :]
    ratios = plane_coeffs[..., 1:, :, :] / plane_coeffs[..., 0:1, :, :]
    height = source.shape[-2]
    breadth = source.shape[-1]
    scaled = source / center

    def operate(field):
        widths = [(0, 0)] * (field.ndim - 2) + [(2, 2), (2, 2)]
        padded = jnp.pad(field, widths)
        result = field
        for number, (step_x, step_y) in enumerate(STENCIL_OFFSETS):
            moved = padded[..., 2 + step_x:2 + step_x + height, 2 + step_y:2 + step_y + breadth]
            result = result - ratios[..., number, :, :][..., None, :, :] * moved
        return result

    sigma = 1.0 / HALF_WIDTH
    rho_old = 1.0 / sigma
    update = scaled
    solution = update
    for sweep_pass in range(passes - 1):
        rho_new = 1.0 / (2.0 * sigma - rho_old)
        residual = scaled - operate(solution)
        update = rho_new * rho_old * update + (2.0 * rho_new / HALF_WIDTH) * residual
        solution = solution + update
        rho_old = rho_new
    return solution


def reference(rhs, coeffs, transmit, counts, elec_x, elec_y):
    slots = rhs.shape[0]
    height = rhs.shape[2]
    breadth = rhs.shape[3]
    index = jnp.arange(slots, dtype=jnp.int32)
    active = (index % CAP) < counts[index // CAP]
    spots = ((jnp.arange(height, dtype=jnp.int32)[None, :, None] == elec_x[:, None, None])
             & (jnp.arange(breadth, dtype=jnp.int32)[None, None, :] == elec_y[:, None, None])).astype(jnp.float32)
    forcing = rhs.at[0].add(INJECTED * spots)

    def downward(carry, item):
        source, local, factor, flag = item
        solved = plane_solve(source, local, CHEB)
        value = jnp.where(flag, solved + factor[None] * carry, 0.0)
        return jnp.where(flag, value, carry), value

    def upward(carry, item):
        field, factor, flag = item
        value = jnp.where(flag, field + factor[None] * carry, 0.0)
        return jnp.where(flag, value, carry), value

    zeros = jnp.zeros(rhs.shape[1:], jnp.float32)
    final_down, forward = lax.scan(downward, zeros, (forcing, coeffs, transmit, active))
    final_up, backward = lax.scan(upward, zeros, (forward, transmit, active), reverse=True)
    return forward, backward
```

```python
import functools

import jax
import jax.numpy as jnp
from jax import lax
from jax.experimental import pallas as pl
from jax.experimental.pallas import tpu as pltpu
from jax.sharding import PartitionSpec as P

CHEB = 4
HALF_WIDTH = 0.72
INJECTED = 4.0
OFFSETS = (
    (1, 0),
    (-1, 0),
    (0, 1),
    (0, -1),
    (2, 0),
    (-2, 0),
    (0, 2),
    (0, -2),
    (1, 1),
    (1, -1),
    (-1, 1),
    (-1, -1),
)
PAD = 8


def cheb_constants(passes):
    sigma = 1.0 / HALF_WIDTH
    rho_old = 1.0 / sigma
    out = []
    for _ in range(passes - 1):
        rho_new = 1.0 / (2.0 * sigma - rho_old)
        out.append((rho_new * rho_old, 2.0 * rho_new / HALF_WIDTH))
        rho_old = rho_new
    return out


def prepare_ratios(coeff, width):
    inverse = 1.0 / coeff[0]
    lane = lax.broadcasted_iota(jnp.int32, inverse.shape, 1)
    groups = {}
    for number, (step_x, step_y) in enumerate(OFFSETS):
        ratio = coeff[number + 1] * inverse
        if step_y:
            inside = (lane + step_y >= 0) & (lane + step_y < width)
            ratio = pltpu.roll(jnp.where(inside, ratio, 0.0), step_y % width, 1)
        groups.setdefault(step_y, []).append((step_x, ratio))
    return inverse, groups


def solve_kernel(
    rhs_hbm, coeff_hbm, transmit_hbm, counts_hbm, ex_hbm, ey_hbm,
    keep_ref, send_ref, solved_ref,
    rhs_v, coeff_v, transmit_v, counts_s, ex_s, ey_s, field, sems,
):
    slots, sources, height, width = rhs_v.shape
    copies = [
        pltpu.make_async_copy(counts_hbm, counts_s, sems.at[0]),
        pltpu.make_async_copy(ex_hbm, ex_s, sems.at[1]),
        pltpu.make_async_copy(ey_hbm, ey_s, sems.at[2]),
        pltpu.make_async_copy(coeff_hbm, coeff_v, sems.at[3]),
        pltpu.make_async_copy(rhs_hbm, rhs_v, sems.at[4]),
        pltpu.make_async_copy(transmit_hbm, transmit_v, sems.at[5]),
    ]
    for copy in copies:
        copy.start()
    position = lax.axis_index("layer")
    zeros = jnp.zeros((PAD, width), jnp.float32)
    for slot in range(slots):
        for source in range(sources):
            field[slot, source, 0:PAD, :] = zeros
            field[slot, source, PAD + height : 2 * PAD + height, :] = zeros
    for copy in copies:
        copy.wait()

    row = lax.broadcasted_iota(jnp.int32, (height, width), 0)
    lane = lax.broadcasted_iota(jnp.int32, (height, width), 1)
    strength = jnp.where(position == 0, INJECTED, 0.0)
    constants = cheb_constants(CHEB)
    for slot in range(slots):
        inverse, groups = prepare_ratios(coeff_v[slot], width)
        for source in range(sources):
            forcing = rhs_v[slot, source]
            if slot == 0:
                at = (row == ex_s[source]) & (lane == ey_s[source])
                forcing = forcing + jnp.where(at, strength, 0.0)
            scaled = forcing * inverse
            update = scaled
            x = scaled
            for number, (momentum, weight) in enumerate(constants):
                field[slot, source, PAD : PAD + height, :] = x
                moved = {0: x}
                for step in (-2, -1, 1, 2):
                    moved[step] = field[slot, source, PAD + step : PAD + step + height, :]
                total = scaled - x
                for step_y, members in groups.items():
                    part = None
                    for step_x, ratio in members:
                        term = ratio * moved[step_x]
                        part = term if part is None else part + term
                    if step_y:
                        part = pltpu.roll(part, (-step_y) % width, 1)
                    total = total + part
                update = momentum * update + weight * total
                x = x + update
            solved_ref[slot, source] = x

    own_count = counts_s[position]
    factors = [transmit_v[slot] for slot in range(slots)]
    flags = [slot < own_count for slot in range(slots)]
    scale = jnp.ones((height, width), jnp.float32)
    responses = []
    for slot in range(slots):
        scale = jnp.where(flags[slot], factors[slot] * scale, scale)
        responses.append(scale)
    bounce = jnp.zeros((height, width), jnp.float32)
    for slot in reversed(range(slots)):
        bounce = jnp.where(flags[slot], responses[slot] + factors[slot] * bounce, bounce)
    left_core = position % 2 == 0

    def put(index, plane):
        top, bottom = plane[: height // 2], plane[height // 2 :]
        keep_ref[index] = jnp.where(left_core, top, bottom)
        send_ref[index] = jnp.where(left_core, bottom, top)

    put(2 * sources, scale)
    put(2 * sources + 1, bounce)
    for source in range(sources):
        down = jnp.zeros((height, width), jnp.float32)
        values = []
        for slot in range(slots):
            down = jnp.where(flags[slot], solved_ref[slot, source] + factors[slot] * down, down)
            values.append(down)
        up = jnp.zeros((height, width), jnp.float32)
        for slot in reversed(range(slots)):
            up = jnp.where(flags[slot], values[slot] + factors[slot] * up, up)
        put(source, down)
        put(sources + source, up)


def split(message):
    sources = (message.shape[0] - 2) // 2
    return (
        message[:sources],
        message[sources : 2 * sources],
        message[2 * sources : 2 * sources + 1],
        message[2 * sources + 1 :],
    )


def merge_kernel(bit, mine_ref, other_ref, out_ref):
    sources = (mine_ref.shape[0] - 2) // 2
    right = (lax.axis_index("layer") & bit) != 0

    def pick(index):
        a, b = mine_ref[index], other_ref[index]
        return jnp.where(right, b, a), jnp.where(right, a, b)

    scale_l, scale_r = pick(2 * sources)
    bounce_l, bounce_r = pick(2 * sources + 1)
    out_ref[2 * sources] = scale_l * scale_r
    out_ref[2 * sources + 1] = bounce_l + scale_l * scale_l * bounce_r
    for source in range(sources):
        down_l, down_r = pick(source)
        up_l, up_r = pick(sources + source)
        out_ref[source] = scale_r * down_l + down_r
        out_ref[sources + source] = up_l + scale_l * (up_r + bounce_r * down_l)


def top_kernel(bit, mine_ref, out_ref):
    sources = (mine_ref.shape[0] - 2) // 2
    right = (lax.axis_index("layer") & bit) != 0
    for source in range(sources):
        out_ref[source] = jnp.where(right, mine_ref[sources + source], mine_ref[source])
    out_ref[sources] = mine_ref[2 * sources + 1]


def down_kernel(levels, *refs):
    own_refs, other_refs, top_ref = refs[:levels], refs[levels : 2 * levels - 1], refs[2 * levels - 1]
    stay_ref, pass_ref = refs[2 * levels], refs[2 * levels + 1]
    sources = (own_refs[0].shape[0] - 2) // 2
    position = lax.axis_index("layer")

    def rights(level):
        return (position & (1 << level)) != 0

    for source in range(sources):
        right = rights(levels - 1)
        own = own_refs[levels - 1]
        got = top_ref[source]
        enter = jnp.where(right, got, 0.0)
        back = jnp.where(right, 0.0, got + top_ref[sources] * own[source])
        for level in reversed(range(levels - 1)):
            right = rights(level)
            own, other = own_refs[level], other_refs[level]

            def pick(index, a=own, b=other, r=right):
                return jnp.where(r, b[index], a[index]), jnp.where(r, a[index], b[index])

            scale_l, scale_r = pick(2 * sources)
            down_l, _ = pick(source)
            _, up_r = pick(sources + source)
            _, bounce_r = pick(2 * sources + 1)
            middle = scale_l * enter + down_l
            above = up_r + bounce_r * middle + scale_r * back
            if level:
                enter = jnp.where(right, middle, enter)
                back = jnp.where(right, back, above)
            else:
                stay_ref[source] = jnp.where(right, middle, enter)
                stay_ref[sources + source] = jnp.where(right, back, above)
                pass_ref[source] = jnp.where(right, enter, middle)
                pass_ref[sources + source] = jnp.where(right, above, back)


def finish_kernel(
    stay_ref, came_ref, solved_ref, transmit_ref, counts_ref, forward_ref, backward_ref
):
    slots, sources, height, width = solved_ref.shape
    position = lax.axis_index("layer")
    left_core = position % 2 == 0
    own_count = counts_ref[position]
    flags = [slot < own_count for slot in range(slots)]
    for source in range(sources):
        for half in range(2):
            rows = slice(half * (height // 2), (half + 1) * (height // 2))
            mine = left_core if half == 0 else jnp.logical_not(left_core)
            down = jnp.where(mine, stay_ref[source], came_ref[source])
            up = jnp.where(mine, stay_ref[sources + source], came_ref[sources + source])
            values = []
            for slot in range(slots):
                value = solved_ref[slot, source, rows, :] + transmit_ref[slot, rows, :] * down
                down = jnp.where(flags[slot], value, down)
                values.append(value)
                forward_ref[slot, source, rows, :] = jnp.where(flags[slot], value, 0.0)
            for slot in reversed(range(slots)):
                value = values[slot] + transmit_ref[slot, rows, :] * up
                up = jnp.where(flags[slot], value, up)
                backward_ref[slot, source, rows, :] = jnp.where(flags[slot], value, 0.0)


VMEM = pl.BlockSpec(memory_space=pltpu.VMEM)
SMEM = pl.BlockSpec(memory_space=pltpu.SMEM)
HBM = pl.BlockSpec(memory_space=pl.ANY)


def call(kernel, out_shapes, *operands, in_specs=None, out_specs=None, **kw):
    shapes = [jax.ShapeDtypeStruct(s, jnp.float32) for s in out_shapes]
    return pl.pallas_call(
        kernel,
        out_shape=shapes,
        in_specs=in_specs or [VMEM] * len(operands),
        out_specs=out_specs or [VMEM] * len(shapes),
        **kw,
    )(*operands)


def local(rhs, coeffs, transmit, counts, elec_x, elec_y):
    slots, sources, height, width = rhs.shape
    devices = lax.axis_size("layer")
    levels = devices.bit_length() - 1
    half = height // 2
    message = (2 * sources + 2, half, width)

    def exchange(x, level):
        bit = 1 << level
        return lax.ppermute(x, "layer", [(i, i ^ bit) for i in range(devices)])

    keep, send, solved = call(
        solve_kernel,
        [message, message, rhs.shape],
        rhs, coeffs, transmit, counts, elec_x, elec_y,
        in_specs=[HBM] * 6,
        scratch_shapes=[
            pltpu.VMEM(rhs.shape, jnp.float32),
            pltpu.VMEM(coeffs.shape, jnp.float32),
            pltpu.VMEM(transmit.shape, jnp.float32),
            pltpu.SMEM(counts.shape, jnp.int32),
            pltpu.SMEM(elec_x.shape, jnp.int32),
            pltpu.SMEM(elec_y.shape, jnp.int32),
            pltpu.VMEM((slots, sources, height + 2 * PAD, width), jnp.float32),
            pltpu.SemaphoreType.DMA((6,)),
        ],
    )
    own, other = [keep], []
    other.append(exchange(send, 0))
    for level in range(1, levels):
        merged, = call(functools.partial(merge_kernel, 1 << (level - 1)), [message], own[-1], other[-1])
        own.append(merged)
        if level < levels - 1:
            other.append(exchange(merged, level))
        else:
            out, = call(
                functools.partial(top_kernel, 1 << level), [(sources + 1, half, width)], merged
            )
            top = exchange(out, level)
    carry = (2 * sources, half, width)
    stay, passed = call(functools.partial(down_kernel, levels), [carry, carry], *own, *other, top)
    came = exchange(passed, 0)
    forward, backward = call(
        finish_kernel,
        [rhs.shape, rhs.shape],
        stay, came, solved, transmit, counts,
        in_specs=[VMEM] * 4 + [SMEM],
    )
    return forward, backward


def solution(mesh):
    placed = (
        P("layer", "grp", None, None),
        P("layer", None, None, None),
        P("layer", None, None),
        P(),
        P("grp"),
        P("grp"),
    )
    return jax.shard_map(
        local,
        mesh=mesh,
        in_specs=placed,
        out_specs=(P("layer", "grp", None, None), P("layer", "grp", None, None)),
        check_vma=False,
    )
```

```python
import functools

import jax
import jax.numpy as jnp
from jax import lax
from jax.experimental import pallas as pl
from jax.experimental.pallas import tpu as pltpu
from jax.sharding import PartitionSpec as P

CHEB = 4
HALF_WIDTH = 0.72
INJECTED = 4.0
OFFSETS = (
    (1, 0),
    (-1, 0),
    (0, 1),
    (0, -1),
    (2, 0),
    (-2, 0),
    (0, 2),
    (0, -2),
    (1, 1),
    (1, -1),
    (-1, 1),
    (-1, -1),
)
PAD = 8
LIMIT = 4 << 20


def cheb_constants(passes):
    sigma = 1.0 / HALF_WIDTH
    rho_old = 1.0 / sigma
    out = []
    for _ in range(passes - 1):
        rho_new = 1.0 / (2.0 * sigma - rho_old)
        out.append((rho_new * rho_old, 2.0 * rho_new / HALF_WIDTH))
        rho_old = rho_new
    return out


def prepare_ratios(coeff, width):
    inverse = 1.0 / coeff[0]
    lane = lax.broadcasted_iota(jnp.int32, inverse.shape, 1)
    groups = {}
    for number, (step_x, step_y) in enumerate(OFFSETS):
        ratio = coeff[number + 1] * inverse
        if step_y:
            inside = (lane + step_y >= 0) & (lane + step_y < width)
            ratio = pltpu.roll(jnp.where(inside, ratio, 0.0), step_y % width, 1)
        groups.setdefault(step_y, []).append((step_x, ratio))
    return inverse, groups


def solve_kernel(
    rhs_hbm, coeff_hbm, transmit_hbm, counts_hbm, ex_hbm, ey_hbm,
    keep_ref, send_ref, solved_ref, factor_ref, active_ref,
    rhs_v, coeff_v, transmit_v, counts_s, ex_s, ey_s, field, sems,
):
    slots, sources, height, width = rhs_v.shape
    copies = [
        pltpu.make_async_copy(counts_hbm, counts_s, sems.at[0]),
        pltpu.make_async_copy(ex_hbm, ex_s, sems.at[1]),
        pltpu.make_async_copy(ey_hbm, ey_s, sems.at[2]),
        pltpu.make_async_copy(coeff_hbm, coeff_v, sems.at[3]),
        pltpu.make_async_copy(rhs_hbm, rhs_v, sems.at[4]),
        pltpu.make_async_copy(transmit_hbm, transmit_v, sems.at[5]),
    ]
    for copy in copies:
        copy.start()
    position = lax.axis_index("layer")
    zeros = jnp.zeros((PAD, width), jnp.float32)
    for slot in range(slots):
        for source in range(sources):
            field[slot, source, 0:PAD, :] = zeros
            field[slot, source, PAD + height : 2 * PAD + height, :] = zeros
    for copy in copies:
        copy.wait()

    row = lax.broadcasted_iota(jnp.int32, (height, width), 0)
    lane = lax.broadcasted_iota(jnp.int32, (height, width), 1)
    strength = jnp.where(position == 0, INJECTED, 0.0)
    constants = cheb_constants(CHEB)
    for slot in range(slots):
        inverse, groups = prepare_ratios(coeff_v[slot], width)
        for source in range(sources):
            forcing = rhs_v[slot, source]
            if slot == 0:
                at = (row == ex_s[source]) & (lane == ey_s[source])
                forcing = forcing + jnp.where(at, strength, 0.0)
            scaled = forcing * inverse
            update = scaled
            x = scaled
            for number, (momentum, weight) in enumerate(constants):
                field[slot, source, PAD : PAD + height, :] = x
                moved = {0: x}
                for step in (-2, -1, 1, 2):
                    moved[step] = field[slot, source, PAD + step : PAD + step + height, :]
                total = scaled - x
                for step_y, members in groups.items():
                    part = None
                    for step_x, ratio in members:
                        term = ratio * moved[step_x]
                        part = term if part is None else part + term
                    if step_y:
                        part = pltpu.roll(part, (-step_y) % width, 1)
                    total = total + part
                update = momentum * update + weight * total
                x = x + update
            solved_ref[slot, source] = x

    own_count = counts_s[position]
    factors = [transmit_v[slot] for slot in range(slots)]
    flags = [slot < own_count for slot in range(slots)]
    for slot in range(slots):
        factor_ref[slot] = factors[slot]
        active_ref[slot] = jnp.where(flags[slot], 1.0, jnp.zeros((height // 2, width), jnp.float32))
    scale = jnp.ones((height, width), jnp.float32)
    responses = []
    for slot in range(slots):
        scale = jnp.where(flags[slot], factors[slot] * scale, scale)
        responses.append(scale)
    bounce = jnp.zeros((height, width), jnp.float32)
    for slot in reversed(range(slots)):
        bounce = jnp.where(flags[slot], responses[slot] + factors[slot] * bounce, bounce)
    left_core = position % 2 == 0

    def put(index, plane):
        top, bottom = plane[: height // 2], plane[height // 2 :]
        keep_ref[index] = jnp.where(left_core, top, bottom)
        send_ref[index] = jnp.where(left_core, bottom, top)

    put(2 * sources, scale)
    put(2 * sources + 1, bounce)
    for source in range(sources):
        down = jnp.zeros((height, width), jnp.float32)
        values = []
        for slot in range(slots):
            down = jnp.where(flags[slot], solved_ref[slot, source] + factors[slot] * down, down)
            values.append(down)
        up = jnp.zeros((height, width), jnp.float32)
        for slot in reversed(range(slots)):
            up = jnp.where(flags[slot], values[slot] + factors[slot] * up, up)
        put(source, down)
        put(sources + source, up)


def split(message):
    sources = (message.shape[0] - 2) // 2
    return (
        message[:sources],
        message[sources : 2 * sources],
        message[2 * sources : 2 * sources + 1],
        message[2 * sources + 1 :],
    )


def merge_kernel(bit, mine_ref, other_ref, out_ref):
    sources = (mine_ref.shape[0] - 2) // 2
    right = (lax.axis_index("layer") & bit) != 0

    def pick(index):
        a, b = mine_ref[index], other_ref[index]
        return jnp.where(right, b, a), jnp.where(right, a, b)

    scale_l, scale_r = pick(2 * sources)
    bounce_l, bounce_r = pick(2 * sources + 1)
    out_ref[2 * sources] = scale_l * scale_r
    out_ref[2 * sources + 1] = bounce_l + scale_l * scale_l * bounce_r
    for source in range(sources):
        down_l, down_r = pick(source)
        up_l, up_r = pick(sources + source)
        out_ref[source] = scale_r * down_l + down_r
        out_ref[sources + source] = up_l + scale_l * (up_r + bounce_r * down_l)


def top_kernel(bit, mine_ref, out_ref):
    sources = (mine_ref.shape[0] - 2) // 2
    right = (lax.axis_index("layer") & bit) != 0
    for source in range(sources):
        out_ref[source] = jnp.where(right, mine_ref[sources + source], mine_ref[source])
    out_ref[sources] = mine_ref[2 * sources + 1]


def down_kernel(levels, *refs):
    own_refs, other_refs, top_ref = refs[:levels], refs[levels : 2 * levels - 1], refs[2 * levels - 1]
    stay_ref, pass_ref = refs[2 * levels], refs[2 * levels + 1]
    sources = (own_refs[0].shape[0] - 2) // 2
    position = lax.axis_index("layer")

    def rights(level):
        return (position & (1 << level)) != 0

    for source in range(sources):
        right = rights(levels - 1)
        own = own_refs[levels - 1]
        got = top_ref[source]
        enter = jnp.where(right, got, 0.0)
        back = jnp.where(right, 0.0, got + top_ref[sources] * own[source])
        for level in reversed(range(levels - 1)):
            right = rights(level)
            own, other = own_refs[level], other_refs[level]

            def pick(index, a=own, b=other, r=right):
                return jnp.where(r, b[index], a[index]), jnp.where(r, a[index], b[index])

            scale_l, scale_r = pick(2 * sources)
            down_l, _ = pick(source)
            _, up_r = pick(sources + source)
            _, bounce_r = pick(2 * sources + 1)
            middle = scale_l * enter + down_l
            above = up_r + bounce_r * middle + scale_r * back
            if level:
                enter = jnp.where(right, middle, enter)
                back = jnp.where(right, back, above)
            else:
                stay_ref[source] = jnp.where(right, middle, enter)
                stay_ref[sources + source] = jnp.where(right, back, above)
                pass_ref[source] = jnp.where(right, enter, middle)
                pass_ref[sources + source] = jnp.where(right, above, back)


def finish_kernel(
    stay_ref, came_ref, solved_ref, transmit_ref, active_ref, forward_ref, backward_ref
):
    slots, sources, height, width = solved_ref.shape
    position = lax.axis_index("layer")
    left_core = position % 2 == 0
    flags = [active_ref[slot] > 0.0 for slot in range(slots)]
    for source in range(sources):
        for half in range(2):
            rows = slice(half * (height // 2), (half + 1) * (height // 2))
            mine = left_core if half == 0 else jnp.logical_not(left_core)
            down = jnp.where(mine, stay_ref[source], came_ref[source])
            up = jnp.where(mine, stay_ref[sources + source], came_ref[sources + source])
            values = []
            for slot in range(slots):
                value = solved_ref[slot, source, rows, :] + transmit_ref[slot, rows, :] * down
                down = jnp.where(flags[slot], value, down)
                values.append(value)
                forward_ref[slot, source, rows, :] = jnp.where(flags[slot], value, 0.0)
            for slot in reversed(range(slots)):
                value = values[slot] + transmit_ref[slot, rows, :] * up
                up = jnp.where(flags[slot], value, up)
                backward_ref[slot, source, rows, :] = jnp.where(flags[slot], value, 0.0)


VMEM = pl.BlockSpec(memory_space=pltpu.VMEM)
HBM = pl.BlockSpec(memory_space=pltpu.HBM)


def call(kernel, out_shapes, *operands, in_specs=None, out_specs=None, **kw):
    shapes = [jax.ShapeDtypeStruct(s, jnp.float32) for s in out_shapes]
    return pl.pallas_call(
        kernel,
        out_shape=shapes,
        in_specs=in_specs or [VMEM] * len(operands),
        out_specs=out_specs or [VMEM] * len(shapes),
        compiler_params=pltpu.CompilerParams(vmem_limit_bytes=LIMIT),
        **kw,
    )(*operands)


def local(rhs, coeffs, transmit, counts, elec_x, elec_y):
    slots, sources, height, width = rhs.shape
    devices = lax.axis_size("layer")
    levels = devices.bit_length() - 1
    half = height // 2
    message = (2 * sources + 2, half, width)

    def exchange(x, level):
        bit = 1 << level
        return lax.ppermute(x, "layer", [(i, i ^ bit) for i in range(devices)])

    keep, send, solved, factor, active = call(
        solve_kernel,
        [message, message, rhs.shape, transmit.shape, (slots, half, width)],
        *(pltpu.with_memory_space_constraint(a, pltpu.HBM) for a in (rhs, coeffs, transmit, counts, elec_x, elec_y)),
        in_specs=[HBM] * 6,
        scratch_shapes=[
            pltpu.VMEM(rhs.shape, jnp.float32),
            pltpu.VMEM(coeffs.shape, jnp.float32),
            pltpu.VMEM(transmit.shape, jnp.float32),
            pltpu.SMEM(counts.shape, jnp.int32),
            pltpu.SMEM(elec_x.shape, jnp.int32),
            pltpu.SMEM(elec_y.shape, jnp.int32),
            pltpu.VMEM((slots, sources, height + 2 * PAD, width), jnp.float32),
            pltpu.SemaphoreType.DMA((6,)),
        ],
    )
    own, other = [keep], []
    other.append(exchange(send, 0))
    for level in range(1, levels):
        merged, = call(functools.partial(merge_kernel, 1 << (level - 1)), [message], own[-1], other[-1])
        own.append(merged)
        if level < levels - 1:
            other.append(exchange(merged, level))
        else:
            out, = call(
                functools.partial(top_kernel, 1 << level), [(sources + 1, half, width)], merged
            )
            top = exchange(out, level)
    carry = (2 * sources, half, width)
    stay, passed = call(functools.partial(down_kernel, levels), [carry, carry], *own, *other, top)
    came = exchange(passed, 0)
    forward, backward = call(
        finish_kernel,
        [rhs.shape, rhs.shape],
        stay, came, solved, factor, active,
    )
    return forward, backward


def solution(mesh):
    placed = (
        P("layer", "grp", None, None),
        P("layer", None, None, None),
        P("layer", None, None),
        P(),
        P("grp"),
        P("grp"),
    )
    return jax.shard_map(
        local,
        mesh=mesh,
        in_specs=placed,
        out_specs=(P("layer", "grp", None, None), P("layer", "grp", None, None)),
        check_vma=False,
    )
```

```python
import functools

import jax
import jax.numpy as jnp
from jax import lax
from jax.experimental import pallas as pl
from jax.experimental.pallas import tpu as pltpu
from jax.sharding import PartitionSpec as P

CHEB = 4
HALF_WIDTH = 0.72
INJECTED = 4.0
OFFSETS = (
    (1, 0),
    (-1, 0),
    (0, 1),
    (0, -1),
    (2, 0),
    (-2, 0),
    (0, 2),
    (0, -2),
    (1, 1),
    (1, -1),
    (-1, 1),
    (-1, -1),
)
PAD = 8
LIMIT = 4 << 20
WIDTH = 2


def cheb_constants(passes):
    sigma = 1.0 / HALF_WIDTH
    rho_old = 1.0 / sigma
    out = []
    for _ in range(passes - 1):
        rho_new = 1.0 / (2.0 * sigma - rho_old)
        out.append((rho_new * rho_old, 2.0 * rho_new / HALF_WIDTH))
        rho_old = rho_new
    return out


def prepare_ratios(coeff, width):
    inverse = 1.0 / coeff[0]
    lane = lax.broadcasted_iota(jnp.int32, inverse.shape, 1)
    groups = {}
    for number, (step_x, step_y) in enumerate(OFFSETS):
        ratio = coeff[number + 1] * inverse
        if step_y:
            inside = (lane + step_y >= 0) & (lane + step_y < width)
            ratio = pltpu.roll(jnp.where(inside, ratio, 0.0), step_y % width, 1)
        groups.setdefault(step_y, []).append((step_x, ratio))
    return inverse, groups


def solve_kernel(
    rhs_hbm, coeff_hbm, transmit_hbm, counts_hbm, ex_hbm, ey_hbm,
    keep_ref, send_ref, solved_ref, factor_ref, active_ref,
    rhs_v, coeff_v, transmit_v, counts_s, ex_s, ey_s, field, sems,
):
    slots, sources, height, width = rhs_v.shape
    copies = [
        pltpu.make_async_copy(counts_hbm, counts_s, sems.at[0]),
        pltpu.make_async_copy(ex_hbm, ex_s, sems.at[1]),
        pltpu.make_async_copy(ey_hbm, ey_s, sems.at[2]),
        pltpu.make_async_copy(coeff_hbm, coeff_v, sems.at[3]),
        pltpu.make_async_copy(rhs_hbm, rhs_v, sems.at[4]),
        pltpu.make_async_copy(transmit_hbm, transmit_v, sems.at[5]),
    ]
    for copy in copies:
        copy.start()
    position = lax.axis_index("layer")
    zeros = jnp.zeros((PAD, width), jnp.float32)
    for slot in range(slots):
        for source in range(sources):
            field[slot, source, 0:PAD, :] = zeros
            field[slot, source, PAD + height : 2 * PAD + height, :] = zeros
    for copy in copies:
        copy.wait()

    row = lax.broadcasted_iota(jnp.int32, (height, width), 0)
    lane = lax.broadcasted_iota(jnp.int32, (height, width), 1)
    strength = jnp.where(position == 0, INJECTED, 0.0)
    constants = cheb_constants(CHEB)
    for slot in range(slots):
        inverse, groups = prepare_ratios(coeff_v[slot], width)
        for source in range(sources):
            forcing = rhs_v[slot, source]
            if slot == 0:
                at = (row == ex_s[source]) & (lane == ey_s[source])
                forcing = forcing + jnp.where(at, strength, 0.0)
            scaled = forcing * inverse
            update = scaled
            x = scaled
            for number, (momentum, weight) in enumerate(constants):
                field[slot, source, PAD : PAD + height, :] = x
                moved = {0: x}
                for step in (-2, -1, 1, 2):
                    moved[step] = field[slot, source, PAD + step : PAD + step + height, :]
                total = scaled - x
                for step_y, members in groups.items():
                    part = None
                    for step_x, ratio in members:
                        term = ratio * moved[step_x]
                        part = term if part is None else part + term
                    if step_y:
                        part = pltpu.roll(part, (-step_y) % width, 1)
                    total = total + part
                update = momentum * update + weight * total
                x = x + update
            solved_ref[slot, source] = x

    own_count = counts_s[position]
    factors = [transmit_v[slot] for slot in range(slots)]
    flags = [slot < own_count for slot in range(slots)]
    for slot in range(slots):
        factor_ref[slot] = factors[slot]
        active_ref[slot] = jnp.where(flags[slot], 1.0, jnp.zeros((height // 2, width), jnp.float32))
    scale = jnp.ones((height, width), jnp.float32)
    responses = []
    for slot in range(slots):
        scale = jnp.where(flags[slot], factors[slot] * scale, scale)
        responses.append(scale)
    bounce = jnp.zeros((height, width), jnp.float32)
    for slot in reversed(range(slots)):
        bounce = jnp.where(flags[slot], responses[slot] + factors[slot] * bounce, bounce)
    left_core = position % 2 == 0

    def put(index, plane):
        top, bottom = plane[: height // 2], plane[height // 2 :]
        keep_ref[index] = jnp.where(left_core, top, bottom)
        send_ref[index] = jnp.where(left_core, bottom, top)

    put(2 * sources, scale)
    put(2 * sources + 1, bounce)
    for source in range(sources):
        down = jnp.zeros((height, width), jnp.float32)
        values = []
        for slot in range(slots):
            down = jnp.where(flags[slot], solved_ref[slot, source] + factors[slot] * down, down)
            values.append(down)
        up = jnp.zeros((height, width), jnp.float32)
        for slot in reversed(range(slots)):
            up = jnp.where(flags[slot], values[slot] + factors[slot] * up, up)
        put(source, down)
        put(sources + source, up)


def bit_of(level):
    return (lax.axis_index("layer") & (1 << level)) != 0


def in_order(items, bits):
    items = list(items)
    for number, bit in enumerate(bits):
        step = 1 << number
        items = [
            jnp.where(bit, items[index ^ step], items[index]) for index in range(len(items))
        ]
    return items


def planes(refs, index, bits):
    return in_order([ref[index] for ref in refs], bits)


def merge_kernel(levels, top, *refs):
    count = 1 << len(levels)
    maps, out_ref = refs[:count], refs[count]
    sources = (out_ref.shape[0] - 2) // 2
    bits = [bit_of(level) for level in levels]
    scales = planes(maps, 2 * sources, bits)
    bounces = planes(maps, 2 * sources + 1, bits)
    scale, bounce = scales[0], bounces[0]
    before = [None]
    for place in range(1, count):
        before.append(scale)
        bounce = bounce + scale * scale * bounces[place]
        scale = scale * scales[place]
    out_ref[2 * sources] = scale
    out_ref[2 * sources + 1] = bounce
    if top is not None:
        right = bit_of(top)
        refs[count + 1][sources] = bounce
    for source in range(sources):
        downs = planes(maps, source, bits)
        ups = planes(maps, sources + source, bits)
        down, up = downs[0], ups[0]
        for place in range(1, count):
            up = up + before[place] * (ups[place] + bounces[place] * down)
            down = scales[place] * down + downs[place]
        out_ref[source] = down
        out_ref[sources + source] = up
        if top is not None:
            refs[count + 1][source] = jnp.where(right, up, down)


def down_kernel(phases, top, *refs):
    refs = list(refs)
    groups = [[refs.pop(0) for _ in range(1 << len(levels))] for levels in phases]
    whole_ref, top_ref, stay_ref, pass_ref = refs
    sources = (whole_ref.shape[0] - 2) // 2
    for source in range(sources):
        right = bit_of(top)
        got = top_ref[source]
        enter = jnp.where(right, got, 0.0)
        back = jnp.where(right, 0.0, got + top_ref[sources] * whole_ref[source])
        for number in reversed(range(len(phases))):
            maps, levels = groups[number], phases[number]
            bits = [bit_of(level) for level in levels]
            scales = planes(maps, 2 * sources, bits)
            bounces = planes(maps, 2 * sources + 1, bits)
            downs = planes(maps, source, bits)
            ups = planes(maps, sources + source, bits)
            enters, backs = [enter], [back]
            for place in range(len(maps) - 1):
                enters.append(scales[place] * enters[-1] + downs[place])
            for place in reversed(range(1, len(maps))):
                backs.append(ups[place] + bounces[place] * enters[place] + scales[place] * backs[-1])
            enters = in_order(enters, bits)
            backs = in_order(backs[::-1], bits)
            enter, back = enters[0], backs[0]
        stay_ref[source], stay_ref[sources + source] = enter, back
        pass_ref[source], pass_ref[sources + source] = enters[1], backs[1]


def finish_kernel(
    stay_ref, came_ref, solved_ref, transmit_ref, active_ref, forward_ref, backward_ref
):
    slots, sources, height, width = solved_ref.shape
    position = lax.axis_index("layer")
    left_core = position % 2 == 0
    flags = [active_ref[slot] > 0.0 for slot in range(slots)]
    for source in range(sources):
        for half in range(2):
            rows = slice(half * (height // 2), (half + 1) * (height // 2))
            mine = left_core if half == 0 else jnp.logical_not(left_core)
            down = jnp.where(mine, stay_ref[source], came_ref[source])
            up = jnp.where(mine, stay_ref[sources + source], came_ref[sources + source])
            values = []
            for slot in range(slots):
                value = solved_ref[slot, source, rows, :] + transmit_ref[slot, rows, :] * down
                down = jnp.where(flags[slot], value, down)
                values.append(value)
                forward_ref[slot, source, rows, :] = jnp.where(flags[slot], value, 0.0)
            for slot in reversed(range(slots)):
                value = values[slot] + transmit_ref[slot, rows, :] * up
                up = jnp.where(flags[slot], value, up)
                backward_ref[slot, source, rows, :] = jnp.where(flags[slot], value, 0.0)


VMEM = pl.BlockSpec(memory_space=pltpu.VMEM)
HBM = pl.BlockSpec(memory_space=pltpu.HBM)


def call(kernel, out_shapes, *operands, in_specs=None, out_specs=None, **kw):
    shapes = [jax.ShapeDtypeStruct(s, jnp.float32) for s in out_shapes]
    return pl.pallas_call(
        kernel,
        out_shape=shapes,
        in_specs=in_specs or [VMEM] * len(operands),
        out_specs=out_specs or [VMEM] * len(shapes),
        compiler_params=pltpu.CompilerParams(vmem_limit_bytes=LIMIT),
        **kw,
    )(*operands)


def local(rhs, coeffs, transmit, counts, elec_x, elec_y):
    slots, sources, height, width = rhs.shape
    devices = lax.axis_size("layer")
    levels = devices.bit_length() - 1
    half = height // 2
    message = (2 * sources + 2, half, width)

    def exchange(x, bit):
        return lax.ppermute(x, "layer", [(i, i ^ bit) for i in range(devices)])

    keep, send, solved, factor, active = call(
        solve_kernel,
        [message, message, rhs.shape, transmit.shape, (slots, half, width)],
        *(pltpu.with_memory_space_constraint(a, pltpu.HBM) for a in (rhs, coeffs, transmit, counts, elec_x, elec_y)),
        in_specs=[HBM] * 6,
        scratch_shapes=[
            pltpu.VMEM(rhs.shape, jnp.float32),
            pltpu.VMEM(coeffs.shape, jnp.float32),
            pltpu.VMEM(transmit.shape, jnp.float32),
            pltpu.SMEM(counts.shape, jnp.int32),
            pltpu.SMEM(elec_x.shape, jnp.int32),
            pltpu.SMEM(elec_y.shape, jnp.int32),
            pltpu.VMEM((slots, sources, height + 2 * PAD, width), jnp.float32),
            pltpu.SemaphoreType.DMA((6,)),
        ],
    )
    top = levels - 1
    phases = [(0,)] + [
        tuple(range(first, min(first + WIDTH, top))) for first in range(1, top, WIDTH)
    ]
    walk, own, sent = [], keep, send
    for number, phase in enumerate(phases):
        maps = [own]
        for index in range(1, 1 << len(phase)):
            maps.append(exchange(sent, index << phase[0]))
        last = number == len(phases) - 1
        own, *extra = call(
            functools.partial(merge_kernel, phase, top if last else None),
            [message] + ([(sources + 1, half, width)] if last else []),
            *maps,
        )
        sent = own
        walk += maps
    got = exchange(extra[0], 1 << top)
    carry = (2 * sources, half, width)
    stay, passed = call(
        functools.partial(down_kernel, phases, top), [carry, carry], *walk, own, got
    )
    came = exchange(passed, 1)
    forward, backward = call(
        finish_kernel,
        [rhs.shape, rhs.shape],
        stay, came, solved, factor, active,
    )
    return forward, backward


def solution(mesh):
    placed = (
        P("layer", "grp", None, None),
        P("layer", None, None, None),
        P("layer", None, None),
        P(),
        P("grp"),
        P("grp"),
    )
    return jax.shard_map(
        local,
        mesh=mesh,
        in_specs=placed,
        out_specs=(P("layer", "grp", None, None), P("layer", "grp", None, None)),
        check_vma=False,
    )
```

```python
import functools

import jax
import jax.numpy as jnp
from jax import lax
from jax.experimental import pallas as pl
from jax.experimental.pallas import tpu as pltpu
from jax.sharding import PartitionSpec as P

CHEB = 4
HALF_WIDTH = 0.72
INJECTED = 4.0
OFFSETS = (
    (1, 0),
    (-1, 0),
    (0, 1),
    (0, -1),
    (2, 0),
    (-2, 0),
    (0, 2),
    (0, -2),
    (1, 1),
    (1, -1),
    (-1, 1),
    (-1, -1),
)
PAD = 8
LIMIT = 4 << 20
WIDTH = 2
CROSSED = (1, 2, 3)


def cheb_constants(passes):
    sigma = 1.0 / HALF_WIDTH
    rho_old = 1.0 / sigma
    out = []
    for _ in range(passes - 1):
        rho_new = 1.0 / (2.0 * sigma - rho_old)
        out.append((rho_new * rho_old, 2.0 * rho_new / HALF_WIDTH))
        rho_old = rho_new
    return out


def prepare_ratios(coeff, width):
    inverse = 1.0 / coeff[0]
    lane = lax.broadcasted_iota(jnp.int32, inverse.shape, 1)
    groups = {}
    for number, (step_x, step_y) in enumerate(OFFSETS):
        ratio = coeff[number + 1] * inverse
        if step_y:
            inside = (lane + step_y >= 0) & (lane + step_y < width)
            ratio = pltpu.roll(jnp.where(inside, ratio, 0.0), step_y % width, 1)
        groups.setdefault(step_y, []).append((step_x, ratio))
    return inverse, groups


def solve_kernel(
    rhs_hbm, coeff_hbm, transmit_hbm, counts_hbm, ex_hbm, ey_hbm,
    keep_ref, send_ref, solved_ref, factor_ref, active_ref,
    rhs_v, coeff_v, transmit_v, counts_s, ex_s, ey_s, field, sems,
):
    slots, sources, height, width = rhs_v.shape
    copies = [
        pltpu.make_async_copy(counts_hbm, counts_s, sems.at[0]),
        pltpu.make_async_copy(ex_hbm, ex_s, sems.at[1]),
        pltpu.make_async_copy(ey_hbm, ey_s, sems.at[2]),
        pltpu.make_async_copy(coeff_hbm, coeff_v, sems.at[3]),
        pltpu.make_async_copy(rhs_hbm, rhs_v, sems.at[4]),
        pltpu.make_async_copy(transmit_hbm, transmit_v, sems.at[5]),
    ]
    for copy in copies:
        copy.start()
    position = lax.axis_index("layer")
    zeros = jnp.zeros((PAD, width), jnp.float32)
    for slot in range(slots):
        for source in range(sources):
            field[slot, source, 0:PAD, :] = zeros
            field[slot, source, PAD + height : 2 * PAD + height, :] = zeros
    for copy in copies:
        copy.wait()

    row = lax.broadcasted_iota(jnp.int32, (height, width), 0)
    lane = lax.broadcasted_iota(jnp.int32, (height, width), 1)
    strength = jnp.where(position == 0, INJECTED, 0.0)
    constants = cheb_constants(CHEB)

    def stencil(slot, source, x, groups):
        field[slot, source, PAD : PAD + height, :] = x
        moved = {0: x}
        for step in (-2, -1, 1, 2):
            moved[step] = field[slot, source, PAD + step : PAD + step + height, :]
        total = None
        for step_y, members in groups.items():
            part = None
            for step_x, ratio in members:
                term = ratio * moved[step_x]
                part = term if part is None else part + term
            if step_y:
                part = pltpu.roll(part, (-step_y) % width, 1)
            total = part if total is None else total + part
        return total

    x, update, scaled, groups = {}, {}, {}, {}
    for slot in range(slots):
        inverse, groups[slot] = prepare_ratios(coeff_v[slot], width)
        for source in range(sources):
            forcing = rhs_v[slot, source]
            if slot == 0:
                at = (row == ex_s[source]) & (lane == ey_s[source])
                forcing = forcing + jnp.where(at, strength, 0.0)
            scaled[slot, source] = forcing * inverse
    x, update = dict(scaled), dict(scaled)
    for number, (momentum, weight) in enumerate(constants):
        for slot in range(slots):
            for source in range(sources):
                k = slot, source
                total = stencil(slot, source, x[k], groups[slot])
                update[k] = momentum * update[k] + weight * (scaled[k] - x[k] + total)
                x[k] = x[k] + update[k]
    for k in x:
        solved_ref[k[0], k[1]] = x[k]

    own_count = counts_s[position]
    factors = [transmit_v[slot] for slot in range(slots)]
    flags = [slot < own_count for slot in range(slots)]
    for slot in range(slots):
        factor_ref[slot] = factors[slot]
        active_ref[slot] = jnp.where(flags[slot], 1.0, jnp.zeros((height // 2, width), jnp.float32))
    scale = jnp.ones((height, width), jnp.float32)
    responses = []
    for slot in range(slots):
        scale = jnp.where(flags[slot], factors[slot] * scale, scale)
        responses.append(scale)
    bounce = jnp.zeros((height, width), jnp.float32)
    for slot in reversed(range(slots)):
        bounce = jnp.where(flags[slot], responses[slot] + factors[slot] * bounce, bounce)
    left_core = half_of(position) == 0

    def put(index, plane):
        top, bottom = plane[: height // 2], plane[height // 2 :]
        keep_ref[index] = jnp.where(left_core, top, bottom)
        send_ref[index] = jnp.where(left_core, bottom, top)

    put(2 * sources, scale)
    put(2 * sources + 1, bounce)
    for source in range(sources):
        down = jnp.zeros((height, width), jnp.float32)
        values = []
        for slot in range(slots):
            down = jnp.where(flags[slot], solved_ref[slot, source] + factors[slot] * down, down)
            values.append(down)
        up = jnp.zeros((height, width), jnp.float32)
        for slot in reversed(range(slots)):
            up = jnp.where(flags[slot], values[slot] + factors[slot] * up, up)
        put(source, down)
        put(sources + source, up)


def half_of(place):
    half = place & 1
    for level in CROSSED:
        half = half ^ ((place >> level) & 1)
    return half


def bit_of(level):
    return (lax.axis_index("layer") & (1 << level)) != 0


def in_order(items, bits):
    items = list(items)
    for number, bit in enumerate(bits):
        step = 1 << number
        items = [
            jnp.where(bit, items[index ^ step], items[index]) for index in range(len(items))
        ]
    return items


def planes(refs, index, bits):
    return in_order([ref[index] for ref in refs], bits)


def merge_kernel(levels, top, *refs):
    count = 1 << len(levels)
    maps, out_ref = refs[:count], refs[count]
    sources = (out_ref.shape[0] - 2) // 2
    bits = [bit_of(level) for level in levels]
    scales = planes(maps, 2 * sources, bits)
    bounces = planes(maps, 2 * sources + 1, bits)
    scale, bounce = scales[0], bounces[0]
    before = [None]
    for place in range(1, count):
        before.append(scale)
        bounce = bounce + scale * scale * bounces[place]
        scale = scale * scales[place]
    out_ref[2 * sources] = scale
    out_ref[2 * sources + 1] = bounce
    if top is not None:
        right = bit_of(top)
        refs[count + 1][sources] = bounce
    for source in range(sources):
        downs = planes(maps, source, bits)
        ups = planes(maps, sources + source, bits)
        down, up = downs[0], ups[0]
        for place in range(1, count):
            up = up + before[place] * (ups[place] + bounces[place] * down)
            down = scales[place] * down + downs[place]
        out_ref[source] = down
        out_ref[sources + source] = up
        if top is not None:
            refs[count + 1][source] = jnp.where(right, up, down)


def down_kernel(phases, top, *refs):
    refs = list(refs)
    groups = [[refs.pop(0) for _ in range(1 << len(levels))] for levels in phases]
    whole_ref, top_ref, stay_ref, pass_ref = refs
    sources = (whole_ref.shape[0] - 2) // 2
    for source in range(sources):
        right = bit_of(top)
        got = top_ref[source]
        enter = jnp.where(right, got, 0.0)
        back = jnp.where(right, 0.0, got + top_ref[sources] * whole_ref[source])
        for number in reversed(range(len(phases))):
            maps, levels = groups[number], phases[number]
            bits = [bit_of(level) for level in levels]
            scales = planes(maps, 2 * sources, bits)
            bounces = planes(maps, 2 * sources + 1, bits)
            downs = planes(maps, source, bits)
            ups = planes(maps, sources + source, bits)
            enters, backs = [enter], [back]
            for place in range(len(maps) - 1):
                enters.append(scales[place] * enters[-1] + downs[place])
            for place in reversed(range(1, len(maps))):
                backs.append(ups[place] + bounces[place] * enters[place] + scales[place] * backs[-1])
            enters = in_order(enters, bits)
            backs = in_order(backs[::-1], bits)
            enter, back = enters[0], backs[0]
        stay_ref[source], stay_ref[sources + source] = enter, back
        pass_ref[source], pass_ref[sources + source] = enters[1], backs[1]


def finish_kernel(
    stay_ref, came_ref, solved_ref, transmit_ref, active_ref, forward_ref, backward_ref
):
    slots, sources, height, width = solved_ref.shape
    left_core = half_of(lax.axis_index("layer")) == 0
    flags = [active_ref[slot] > 0.0 for slot in range(slots)]
    for source in range(sources):
        for half in range(2):
            rows = slice(half * (height // 2), (half + 1) * (height // 2))
            mine = left_core if half == 0 else jnp.logical_not(left_core)
            down = jnp.where(mine, stay_ref[source], came_ref[source])
            up = jnp.where(mine, stay_ref[sources + source], came_ref[sources + source])
            values = []
            for slot in range(slots):
                value = solved_ref[slot, source, rows, :] + transmit_ref[slot, rows, :] * down
                down = jnp.where(flags[slot], value, down)
                values.append(value)
                forward_ref[slot, source, rows, :] = jnp.where(flags[slot], value, 0.0)
            for slot in reversed(range(slots)):
                value = values[slot] + transmit_ref[slot, rows, :] * up
                up = jnp.where(flags[slot], value, up)
                backward_ref[slot, source, rows, :] = jnp.where(flags[slot], value, 0.0)


VMEM = pl.BlockSpec(memory_space=pltpu.VMEM)
HBM = pl.BlockSpec(memory_space=pltpu.HBM)


def call(kernel, out_shapes, *operands, in_specs=None, out_specs=None, **kw):
    shapes = [jax.ShapeDtypeStruct(s, jnp.float32) for s in out_shapes]
    return pl.pallas_call(
        kernel,
        out_shape=shapes,
        in_specs=in_specs or [VMEM] * len(operands),
        out_specs=out_specs or [VMEM] * len(shapes),
        compiler_params=pltpu.CompilerParams(vmem_limit_bytes=LIMIT),
        **kw,
    )(*operands)


def local(rhs, coeffs, transmit, counts, elec_x, elec_y):
    slots, sources, height, width = rhs.shape
    devices = lax.axis_size("layer")
    levels = devices.bit_length() - 1
    half = height // 2
    message = (2 * sources + 2, half, width)

    def exchange(x, bit):
        other = bit ^ half_of(bit & -2)
        return lax.ppermute(x, "layer", [(i, i ^ other) for i in range(devices)])

    keep, send, solved, factor, active = call(
        solve_kernel,
        [message, message, rhs.shape, transmit.shape, (slots, half, width)],
        *(pltpu.with_memory_space_constraint(a, pltpu.HBM) for a in (rhs, coeffs, transmit, counts, elec_x, elec_y)),
        in_specs=[HBM] * 6,
        scratch_shapes=[
            pltpu.VMEM(rhs.shape, jnp.float32),
            pltpu.VMEM(coeffs.shape, jnp.float32),
            pltpu.VMEM(transmit.shape, jnp.float32),
            pltpu.SMEM(counts.shape, jnp.int32),
            pltpu.SMEM(elec_x.shape, jnp.int32),
            pltpu.SMEM(elec_y.shape, jnp.int32),
            pltpu.VMEM((slots, sources, height + 2 * PAD, width), jnp.float32),
            pltpu.SemaphoreType.DMA((6,)),
        ],
    )
    top = levels - 1
    phases = [(0,)] + [
        tuple(range(first, min(first + WIDTH, top))) for first in range(1, top, WIDTH)
    ]
    walk, own, sent = [], keep, send
    for number, phase in enumerate(phases):
        maps = [own]
        for index in range(1, 1 << len(phase)):
            maps.append(exchange(sent, index << phase[0]))
        last = number == len(phases) - 1
        own, *extra = call(
            functools.partial(merge_kernel, phase, top if last else None),
            [message] + ([(sources + 1, half, width)] if last else []),
            *maps,
        )
        sent = own
        walk += maps
    got = exchange(extra[0], 1 << top)
    carry = (2 * sources, half, width)
    stay, passed = call(
        functools.partial(down_kernel, phases, top), [carry, carry], *walk, own, got
    )
    came = exchange(passed, 1)
    forward, backward = call(
        finish_kernel,
        [rhs.shape, rhs.shape],
        stay, came, solved, factor, active,
    )
    return forward, backward


def solution(mesh):
    placed = (
        P("layer", "grp", None, None),
        P("layer", None, None, None),
        P("layer", None, None),
        P(),
        P("grp"),
        P("grp"),
    )
    return jax.shard_map(
        local,
        mesh=mesh,
        in_specs=placed,
        out_specs=(P("layer", "grp", None, None), P("layer", "grp", None, None)),
        check_vma=False,
    )
```

```python
import functools

import jax
import jax.numpy as jnp
from jax import lax
from jax.experimental import pallas as pl
from jax.experimental.pallas import tpu as pltpu
from jax.sharding import PartitionSpec as P

CHEB = 4
HALF_WIDTH = 0.72
INJECTED = 4.0
OFFSETS = (
    (1, 0),
    (-1, 0),
    (0, 1),
    (0, -1),
    (2, 0),
    (-2, 0),
    (0, 2),
    (0, -2),
    (1, 1),
    (1, -1),
    (-1, 1),
    (-1, -1),
)
PAD = 8
LIMIT = 4 << 20
WIDTH = 2
CROSSED = (1, 2, 3)


def cheb_constants(passes):
    sigma = 1.0 / HALF_WIDTH
    rho_old = 1.0 / sigma
    out = []
    for _ in range(passes - 1):
        rho_new = 1.0 / (2.0 * sigma - rho_old)
        out.append((rho_new * rho_old, 2.0 * rho_new / HALF_WIDTH))
        rho_old = rho_new
    return out


def prepare_ratios(coeff, width):
    inverse = 1.0 / coeff[0]
    lane = lax.broadcasted_iota(jnp.int32, inverse.shape, 1)
    groups = {}
    for number, (step_x, step_y) in enumerate(OFFSETS):
        ratio = coeff[number + 1] * inverse
        if step_y:
            inside = (lane + step_y >= 0) & (lane + step_y < width)
            ratio = pltpu.roll(jnp.where(inside, ratio, 0.0), step_y % width, 1)
        groups.setdefault(step_y, []).append((step_x, ratio))
    return inverse, groups


def solve_kernel(
    rhs_hbm, coeff_hbm, transmit_hbm, counts_hbm, ex_hbm, ey_hbm,
    keep_ref, send_ref, solved_ref, factor_ref, active_ref,
    rhs_v, coeff_v, transmit_v, counts_s, ex_s, ey_s, field, sems,
):
    slots, sources, height, width = rhs_v.shape
    copies = [
        pltpu.make_async_copy(counts_hbm, counts_s, sems.at[0]),
        pltpu.make_async_copy(ex_hbm, ex_s, sems.at[1]),
        pltpu.make_async_copy(ey_hbm, ey_s, sems.at[2]),
        pltpu.make_async_copy(coeff_hbm, coeff_v, sems.at[3]),
        pltpu.make_async_copy(rhs_hbm, rhs_v, sems.at[4]),
        pltpu.make_async_copy(transmit_hbm, transmit_v, sems.at[5]),
    ]
    for copy in copies:
        copy.start()
    position = lax.axis_index("layer")
    zeros = jnp.zeros((PAD, width), jnp.float32)
    for slot in range(slots):
        for source in range(sources):
            field[slot, source, 0:PAD, :] = zeros
            field[slot, source, PAD + height : 2 * PAD + height, :] = zeros
    for copy in copies:
        copy.wait()

    row = lax.broadcasted_iota(jnp.int32, (height, width), 0)
    lane = lax.broadcasted_iota(jnp.int32, (height, width), 1)
    strength = jnp.where(position == 0, INJECTED, 0.0)
    constants = cheb_constants(CHEB)

    def stencil(slot, source, x, groups):
        field[slot, source, PAD : PAD + height, :] = x
        moved = {0: x}
        for step in (-2, -1, 1, 2):
            moved[step] = field[slot, source, PAD + step : PAD + step + height, :]
        total = None
        for step_y, members in groups.items():
            part = None
            for step_x, ratio in members:
                term = ratio * moved[step_x]
                part = term if part is None else part + term
            if step_y:
                part = pltpu.roll(part, (-step_y) % width, 1)
            total = part if total is None else total + part
        return total

    x, update, scaled, groups = {}, {}, {}, {}
    for slot in range(slots):
        inverse, groups[slot] = prepare_ratios(coeff_v[slot], width)
        for source in range(sources):
            forcing = rhs_v[slot, source]
            if slot == 0:
                at = (row == ex_s[source]) & (lane == ey_s[source])
                forcing = forcing + jnp.where(at, strength, 0.0)
            scaled[slot, source] = forcing * inverse
    x, update = dict(scaled), dict(scaled)
    for number, (momentum, weight) in enumerate(constants):
        for slot in range(slots):
            for source in range(sources):
                k = slot, source
                total = stencil(slot, source, x[k], groups[slot])
                update[k] = momentum * update[k] + weight * (scaled[k] - x[k] + total)
                x[k] = x[k] + update[k]
    for k in x:
        solved_ref[k[0], k[1]] = x[k]

    own_count = counts_s[position]
    factors = [transmit_v[slot] for slot in range(slots)]
    flags = [slot < own_count for slot in range(slots)]
    for slot in range(slots):
        factor_ref[slot] = factors[slot]
        active_ref[slot] = jnp.where(flags[slot], 1.0, jnp.zeros((height // 2, width), jnp.float32))
    scale = jnp.ones((height, width), jnp.float32)
    responses = []
    for slot in range(slots):
        scale = jnp.where(flags[slot], factors[slot] * scale, scale)
        responses.append(scale)
    bounce = jnp.zeros((height, width), jnp.float32)
    for slot in reversed(range(slots)):
        bounce = jnp.where(flags[slot], responses[slot] + factors[slot] * bounce, bounce)
    left_core = half_of(position) == 0

    def put(index, plane):
        top, bottom = plane[: height // 2], plane[height // 2 :]
        keep_ref[index] = jnp.where(left_core, top, bottom)
        send_ref[index] = jnp.where(left_core, bottom, top)

    put(2 * sources, scale)
    put(2 * sources + 1, bounce)
    for source in range(sources):
        down = jnp.zeros((height, width), jnp.float32)
        values = []
        for slot in range(slots):
            down = jnp.where(flags[slot], solved_ref[slot, source] + factors[slot] * down, down)
            values.append(down)
        up = jnp.zeros((height, width), jnp.float32)
        for slot in reversed(range(slots)):
            up = jnp.where(flags[slot], values[slot] + factors[slot] * up, up)
        put(source, down)
        put(sources + source, up)


def half_of(place):
    half = place & 1
    for level in CROSSED:
        half = half ^ ((place >> level) & 1)
    return half


def bit_of(level):
    return (lax.axis_index("layer") & (1 << level)) != 0


def in_order(items, bits):
    items = list(items)
    for number, bit in enumerate(bits):
        step = 1 << number
        items = [
            jnp.where(bit, items[index ^ step], items[index]) for index in range(len(items))
        ]
    return items


def planes(refs, index, bits):
    return in_order([ref[index] for ref in refs], bits)


def merge_kernel(levels, top, *refs):
    count = 1 << len(levels)
    maps, out_ref = refs[:count], refs[count]
    sources = (out_ref.shape[0] - 2) // 2
    bits = [bit_of(level) for level in levels]
    scales = planes(maps, 2 * sources, bits)
    bounces = planes(maps, 2 * sources + 1, bits)
    scale, bounce = scales[0], bounces[0]
    before = [None]
    for place in range(1, count):
        before.append(scale)
        bounce = bounce + scale * scale * bounces[place]
        scale = scale * scales[place]
    out_ref[2 * sources] = scale
    out_ref[2 * sources + 1] = bounce
    if top is not None:
        right = bit_of(top)
        refs[count + 1][sources] = bounce
    for source in range(sources):
        downs = planes(maps, source, bits)
        ups = planes(maps, sources + source, bits)
        down, up = downs[0], ups[0]
        for place in range(1, count):
            up = up + before[place] * (ups[place] + bounces[place] * down)
            down = scales[place] * down + downs[place]
        out_ref[source] = down
        out_ref[sources + source] = up
        if top is not None:
            refs[count + 1][source] = jnp.where(right, up, down)


def prepare_kernel(phases, top, *refs):
    refs = list(refs)
    groups = [[refs.pop(0) for _ in range(1 << len(levels))] for levels in phases]
    whole_ref, out_ref = refs
    sources = (whole_ref.shape[0] - 2) // 2
    right = bit_of(top)

    def walk(source):
        if source is None:
            enter, back = (1.0,), (0.0, 1.0)
        else:
            enter, back = (0.0,), (0.0,)
        for number in reversed(range(len(phases))):
            maps, levels = groups[number], phases[number]
            bits = [bit_of(level) for level in levels]
            scales = planes(maps, 2 * sources, bits)
            bounces = planes(maps, 2 * sources + 1, bits)
            if source is not None:
                downs = planes(maps, source, bits)
                ups = planes(maps, sources + source, bits)
            enters, backs = [enter], [back]
            for place in range(len(maps) - 1):
                value = scales[place] * enters[-1][0]
                enters.append((value if source is None else value + downs[place],))
            for place in reversed(range(1, len(maps))):
                value = bounces[place] * enters[place][0] + scales[place] * backs[-1][0]
                if source is None:
                    backs.append((value, scales[place] * backs[-1][1]))
                else:
                    backs.append((ups[place] + value,))
            enters = list(zip(*(in_order(part, bits) for part in zip(*enters))))
            backs = list(zip(*(in_order(part, bits) for part in zip(*backs[::-1]))))
            enter, back = enters[0], backs[0]
        return enters[:2], backs[:2]

    enters, backs = walk(None)
    through = []
    for who in range(2):
        (alpha,), (delta, epsilon) = enters[who], backs[who]
        out_ref[who, 3 * sources] = jnp.where(right, alpha, 0.0)
        out_ref[who, 3 * sources + 1] = jnp.where(right, delta, epsilon)
        through.append(jnp.where(right, 0.0, epsilon))
    for source in range(sources):
        enters, backs = walk(source)
        for who in range(2):
            out_ref[who, source] = enters[who][0]
            out_ref[who, sources + source] = backs[who][0]
            out_ref[who, 2 * sources + source] = through[who] * whole_ref[source]


def down_kernel(form_ref, top_ref, stay_ref, pass_ref):
    sources = stay_ref.shape[0] // 2
    bounce = top_ref[sources]
    for who, out_ref in ((1, pass_ref), (0, stay_ref)):
        down, up = form_ref[who, 3 * sources], form_ref[who, 3 * sources + 1]
        for source in range(sources):
            got = top_ref[source]
            out_ref[source] = form_ref[who, source] + down * got
            out_ref[sources + source] = (
                form_ref[who, sources + source]
                + up * got
                + form_ref[who, 2 * sources + source] * bounce
            )


def finish_kernel(
    offset, carry_ref, solved_ref, transmit_ref, active_ref, *refs
):
    forward_hbm, backward_hbm, forward_ref, backward_ref, sems = refs[-5:]
    slots, sources, half, width = forward_ref.shape
    which = half_of(lax.axis_index("layer")) ^ offset
    rows = pl.ds(pl.multiple_of(which * half, half), half)
    flags = [active_ref[slot] > 0.0 for slot in range(slots)]
    factors = [transmit_ref[slot, rows, :] for slot in range(slots)]
    for source in range(sources):
        down, up = carry_ref[source], carry_ref[sources + source]
        values = []
        for slot in range(slots):
            value = solved_ref[slot, source, rows, :] + factors[slot] * down
            down = jnp.where(flags[slot], value, down)
            values.append(value)
            forward_ref[slot, source] = jnp.where(flags[slot], value, 0.0)
        for slot in reversed(range(slots)):
            value = values[slot] + factors[slot] * up
            up = jnp.where(flags[slot], value, up)
            backward_ref[slot, source] = jnp.where(flags[slot], value, 0.0)
    copies = [
        pltpu.make_async_copy(forward_ref, forward_hbm.at[:, :, rows, :], sems.at[0]),
        pltpu.make_async_copy(backward_ref, backward_hbm.at[:, :, rows, :], sems.at[1]),
    ]
    for copy in copies:
        copy.start()
    for copy in copies:
        copy.wait()


VMEM = pl.BlockSpec(memory_space=pltpu.VMEM)
HBM = pl.BlockSpec(memory_space=pltpu.HBM)


def call(kernel, out_shapes, *operands, in_specs=None, out_specs=None, **kw):
    shapes = [jax.ShapeDtypeStruct(s, jnp.float32) for s in out_shapes]
    return pl.pallas_call(
        kernel,
        out_shape=shapes,
        in_specs=in_specs or [VMEM] * len(operands),
        out_specs=out_specs or [VMEM] * len(shapes),
        compiler_params=pltpu.CompilerParams(vmem_limit_bytes=LIMIT),
        **kw,
    )(*operands)


def local(rhs, coeffs, transmit, counts, elec_x, elec_y):
    slots, sources, height, width = rhs.shape
    devices = lax.axis_size("layer")
    levels = devices.bit_length() - 1
    half = height // 2
    message = (2 * sources + 2, half, width)

    def exchange(x, bit):
        other = bit ^ half_of(bit & -2)
        return lax.ppermute(x, "layer", [(i, i ^ other) for i in range(devices)])

    keep, send, solved, factor, active = call(
        solve_kernel,
        [message, message, rhs.shape, transmit.shape, (slots, half, width)],
        *(pltpu.with_memory_space_constraint(a, pltpu.HBM) for a in (rhs, coeffs, transmit, counts, elec_x, elec_y)),
        in_specs=[HBM] * 6,
        scratch_shapes=[
            pltpu.VMEM(rhs.shape, jnp.float32),
            pltpu.VMEM(coeffs.shape, jnp.float32),
            pltpu.VMEM(transmit.shape, jnp.float32),
            pltpu.SMEM(counts.shape, jnp.int32),
            pltpu.SMEM(elec_x.shape, jnp.int32),
            pltpu.SMEM(elec_y.shape, jnp.int32),
            pltpu.VMEM((slots, sources, height + 2 * PAD, width), jnp.float32),
            pltpu.SemaphoreType.DMA((6,)),
        ],
    )
    top = levels - 1
    phases = [(0,)] + [
        tuple(range(first, min(first + WIDTH, top))) for first in range(1, top, WIDTH)
    ]
    walk, own, sent = [], keep, send
    for number, phase in enumerate(phases):
        maps = [own]
        for index in range(1, 1 << len(phase)):
            maps.append(exchange(sent, index << phase[0]))
        last = number == len(phases) - 1
        own, *extra = call(
            functools.partial(merge_kernel, phase, top if last else None),
            [message] + ([(sources + 1, half, width)] if last else []),
            *maps,
        )
        sent = own
        walk += maps
    got = exchange(extra[0], 1 << top)
    carry = (2 * sources, half, width)
    form, = call(
        functools.partial(prepare_kernel, phases, top),
        [(2, 3 * sources + 2, half, width)],
        *walk, own,
    )
    stay, passed = call(down_kernel, [carry, carry], form, got)
    came = exchange(passed, 1)

    def finish(offset, carried, *earlier):
        return call(
            functools.partial(finish_kernel, offset),
            [rhs.shape, rhs.shape],
            carried, solved, factor, active,
            *(pltpu.with_memory_space_constraint(e, pltpu.HBM) for e in earlier),
            in_specs=[VMEM] * 4 + [HBM] * len(earlier),
            out_specs=[HBM] * 2,
            scratch_shapes=[
                pltpu.VMEM((slots, sources, half, width), jnp.float32),
                pltpu.VMEM((slots, sources, half, width), jnp.float32),
                pltpu.SemaphoreType.DMA((2,)),
            ],
            input_output_aliases={4 + n: n for n in range(len(earlier))},
        )

    forward, backward = finish(1, came, *finish(0, stay))
    return forward, backward


def solution(mesh):
    placed = (
        P("layer", "grp", None, None),
        P("layer", None, None, None),
        P("layer", None, None),
        P(),
        P("grp"),
        P("grp"),
    )
    return jax.shard_map(
        local,
        mesh=mesh,
        in_specs=placed,
        out_specs=(P("layer", "grp", None, None), P("layer", "grp", None, None)),
        check_vma=False,
    )
```

```python
import functools

import jax
import jax.numpy as jnp
from jax import lax
from jax.experimental import pallas as pl
from jax.experimental.pallas import tpu as pltpu
from jax.sharding import PartitionSpec as P

CHEB = 4
HALF_WIDTH = 0.72
INJECTED = 4.0
OFFSETS = (
    (1, 0),
    (-1, 0),
    (0, 1),
    (0, -1),
    (2, 0),
    (-2, 0),
    (0, 2),
    (0, -2),
    (1, 1),
    (1, -1),
    (-1, 1),
    (-1, -1),
)
PAD = 8
LIMIT = 4 << 20
WIDTH = 2
TURN = (1, 2, 0)
CROSSED = (1, 2, 3)


def cheb_constants(passes):
    sigma = 1.0 / HALF_WIDTH
    rho_old = 1.0 / sigma
    out = []
    for _ in range(passes - 1):
        rho_new = 1.0 / (2.0 * sigma - rho_old)
        out.append((rho_new * rho_old, 2.0 * rho_new / HALF_WIDTH))
        rho_old = rho_new
    return out


def prepare_ratios(coeff, width):
    inverse = 1.0 / coeff[0]
    lane = lax.broadcasted_iota(jnp.int32, inverse.shape, 1)
    groups = {}
    for number, (step_x, step_y) in enumerate(OFFSETS):
        ratio = coeff[number + 1] * inverse
        if step_y:
            inside = (lane + step_y >= 0) & (lane + step_y < width)
            ratio = pltpu.roll(jnp.where(inside, ratio, 0.0), step_y % width, 1)
        groups.setdefault(step_y, []).append((step_x, ratio))
    return inverse, groups


def solve_kernel(
    rhs_hbm, coeff_hbm, transmit_hbm, counts_hbm, ex_hbm, ey_hbm,
    keep_ref, send_ref, solved_ref, factor_ref, active_ref,
    rhs_v, coeff_v, transmit_v, counts_s, ex_s, ey_s, field, sems,
):
    slots, sources, height, width = rhs_v.shape
    copies = [
        pltpu.make_async_copy(counts_hbm, counts_s, sems.at[0]),
        pltpu.make_async_copy(ex_hbm, ex_s, sems.at[1]),
        pltpu.make_async_copy(ey_hbm, ey_s, sems.at[2]),
        pltpu.make_async_copy(coeff_hbm, coeff_v, sems.at[3]),
        pltpu.make_async_copy(rhs_hbm, rhs_v, sems.at[4]),
        pltpu.make_async_copy(transmit_hbm, transmit_v, sems.at[5]),
    ]
    for copy in copies:
        copy.start()
    position = lax.axis_index("layer")
    zeros = jnp.zeros((PAD, width), jnp.float32)
    for slot in range(slots):
        for source in range(sources):
            field[slot, source, 0:PAD, :] = zeros
            field[slot, source, PAD + height : 2 * PAD + height, :] = zeros
    for copy in copies:
        copy.wait()

    row = lax.broadcasted_iota(jnp.int32, (height, width), 0)
    lane = lax.broadcasted_iota(jnp.int32, (height, width), 1)
    strength = jnp.where(position == 0, INJECTED, 0.0)
    constants = cheb_constants(CHEB)

    def stencil(slot, source, x, groups):
        field[slot, source, PAD : PAD + height, :] = x
        moved = {0: x}
        for step in (-2, -1, 1, 2):
            moved[step] = field[slot, source, PAD + step : PAD + step + height, :]
        total = None
        for step_y, members in groups.items():
            part = None
            for step_x, ratio in members:
                term = ratio * moved[step_x]
                part = term if part is None else part + term
            if step_y:
                part = pltpu.roll(part, (-step_y) % width, 1)
            total = part if total is None else total + part
        return total

    x, update, scaled, groups = {}, {}, {}, {}
    for slot in range(slots):
        inverse, groups[slot] = prepare_ratios(coeff_v[slot], width)
        for source in range(sources):
            forcing = rhs_v[slot, source]
            if slot == 0:
                at = (row == ex_s[source]) & (lane == ey_s[source])
                forcing = forcing + jnp.where(at, strength, 0.0)
            scaled[slot, source] = forcing * inverse
    x, update = dict(scaled), dict(scaled)
    for number, (momentum, weight) in enumerate(constants):
        for slot in range(slots):
            for source in range(sources):
                k = slot, source
                total = stencil(slot, source, x[k], groups[slot])
                update[k] = momentum * update[k] + weight * (scaled[k] - x[k] + total)
                x[k] = x[k] + update[k]
    for k in x:
        solved_ref[k[0], k[1]] = x[k]

    own_count = counts_s[position]
    factors = [transmit_v[slot] for slot in range(slots)]
    flags = [slot < own_count for slot in range(slots)]
    for slot in range(slots):
        factor_ref[slot] = factors[slot]
        active_ref[slot] = jnp.where(flags[slot], 1.0, jnp.zeros((height // 2, width), jnp.float32))
    scale = jnp.ones((height, width), jnp.float32)
    responses = []
    for slot in range(slots):
        scale = jnp.where(flags[slot], factors[slot] * scale, scale)
        responses.append(scale)
    bounce = jnp.zeros((height, width), jnp.float32)
    for slot in reversed(range(slots)):
        bounce = jnp.where(flags[slot], responses[slot] + factors[slot] * bounce, bounce)
    left_core = half_of(position) == 0

    def put(index, plane):
        top, bottom = plane[: height // 2], plane[height // 2 :]
        keep_ref[index] = jnp.where(left_core, top, bottom)
        send_ref[index] = jnp.where(left_core, bottom, top)

    put(2 * sources, scale)
    put(2 * sources + 1, bounce)
    for source in range(sources):
        down = jnp.zeros((height, width), jnp.float32)
        values = []
        for slot in range(slots):
            down = jnp.where(flags[slot], solved_ref[slot, source] + factors[slot] * down, down)
            values.append(down)
        up = jnp.zeros((height, width), jnp.float32)
        for slot in reversed(range(slots)):
            up = jnp.where(flags[slot], values[slot] + factors[slot] * up, up)
        put(source, down)
        put(sources + source, up)


def half_of(place):
    half = place & 1
    for level in CROSSED:
        half = half ^ ((place >> level) & 1)
    return half


def bit_of(level):
    return (lax.axis_index("layer") & (1 << level)) != 0


def in_order(items, bits):
    items = list(items)
    for number, bit in enumerate(bits):
        step = 1 << number
        items = [
            jnp.where(bit, items[index ^ step], items[index]) for index in range(len(items))
        ]
    return items


def planes(refs, index, bits):
    own, *others = [ref[index] for ref in refs]
    if len(others) == 3:
        second = half_of(lax.axis_index("layer")) == 1
        others = [jnp.where(second, others[TURN.index(k)], others[k]) for k in range(3)]
    return in_order([own] + others, bits)


def merge_kernel(levels, top, *refs):
    count = 1 << len(levels)
    maps, out_ref = refs[:count], refs[count]
    sources = (out_ref.shape[0] - 2) // 2
    bits = [bit_of(level) for level in levels]
    scales = planes(maps, 2 * sources, bits)
    bounces = planes(maps, 2 * sources + 1, bits)
    scale, bounce = scales[0], bounces[0]
    before = [None]
    for place in range(1, count):
        before.append(scale)
        bounce = bounce + scale * scale * bounces[place]
        scale = scale * scales[place]
    out_ref[2 * sources] = scale
    out_ref[2 * sources + 1] = bounce
    if top is not None:
        right = bit_of(top)
        refs[count + 1][sources] = bounce
    for source in range(sources):
        downs = planes(maps, source, bits)
        ups = planes(maps, sources + source, bits)
        down, up = downs[0], ups[0]
        for place in range(1, count):
            up = up + before[place] * (ups[place] + bounces[place] * down)
            down = scales[place] * down + downs[place]
        out_ref[source] = down
        out_ref[sources + source] = up
        if top is not None:
            refs[count + 1][source] = jnp.where(right, up, down)


def prepare_kernel(phases, top, *refs):
    refs = list(refs)
    groups = [[refs.pop(0) for _ in range(1 << len(levels))] for levels in phases]
    whole_ref, out_ref = refs
    sources = (whole_ref.shape[0] - 2) // 2
    right = bit_of(top)

    def walk(source):
        if source is None:
            enter, back = (1.0,), (0.0, 1.0)
        else:
            enter, back = (0.0,), (0.0,)
        for number in reversed(range(len(phases))):
            maps, levels = groups[number], phases[number]
            bits = [bit_of(level) for level in levels]
            scales = planes(maps, 2 * sources, bits)
            bounces = planes(maps, 2 * sources + 1, bits)
            if source is not None:
                downs = planes(maps, source, bits)
                ups = planes(maps, sources + source, bits)
            enters, backs = [enter], [back]
            for place in range(len(maps) - 1):
                value = scales[place] * enters[-1][0]
                enters.append((value if source is None else value + downs[place],))
            for place in reversed(range(1, len(maps))):
                value = bounces[place] * enters[place][0] + scales[place] * backs[-1][0]
                if source is None:
                    backs.append((value, scales[place] * backs[-1][1]))
                else:
                    backs.append((ups[place] + value,))
            enters = list(zip(*(in_order(part, bits) for part in zip(*enters))))
            backs = list(zip(*(in_order(part, bits) for part in zip(*backs[::-1]))))
            enter, back = enters[0], backs[0]
        return enters[:2], backs[:2]

    enters, backs = walk(None)
    through = []
    for who in range(2):
        (alpha,), (delta, epsilon) = enters[who], backs[who]
        out_ref[who, 3 * sources] = jnp.where(right, alpha, 0.0)
        out_ref[who, 3 * sources + 1] = jnp.where(right, delta, epsilon)
        through.append(jnp.where(right, 0.0, epsilon))
    for source in range(sources):
        enters, backs = walk(source)
        for who in range(2):
            out_ref[who, source] = enters[who][0]
            out_ref[who, sources + source] = backs[who][0]
            out_ref[who, 2 * sources + source] = through[who] * whole_ref[source]


def down_kernel(form_ref, top_ref, stay_ref, pass_ref):
    sources = stay_ref.shape[0] // 2
    bounce = top_ref[sources]
    for who, out_ref in ((1, pass_ref), (0, stay_ref)):
        down, up = form_ref[who, 3 * sources], form_ref[who, 3 * sources + 1]
        for source in range(sources):
            got = top_ref[source]
            out_ref[source] = form_ref[who, source] + down * got
            out_ref[sources + source] = (
                form_ref[who, sources + source]
                + up * got
                + form_ref[who, 2 * sources + source] * bounce
            )


def finish_kernel(
    offset, carry_ref, solved_ref, transmit_ref, active_ref, *refs
):
    forward_hbm, backward_hbm, forward_ref, backward_ref, sems = refs[-5:]
    slots, sources, half, width = forward_ref.shape
    which = half_of(lax.axis_index("layer")) ^ offset
    rows = pl.ds(pl.multiple_of(which * half, half), half)
    flags = [active_ref[slot] > 0.0 for slot in range(slots)]
    factors = [transmit_ref[slot, rows, :] for slot in range(slots)]
    for source in range(sources):
        down, up = carry_ref[source], carry_ref[sources + source]
        values = []
        for slot in range(slots):
            value = solved_ref[slot, source, rows, :] + factors[slot] * down
            down = jnp.where(flags[slot], value, down)
            values.append(value)
            forward_ref[slot, source] = jnp.where(flags[slot], value, 0.0)
        for slot in reversed(range(slots)):
            value = values[slot] + factors[slot] * up
            up = jnp.where(flags[slot], value, up)
            backward_ref[slot, source] = jnp.where(flags[slot], value, 0.0)
    copies = [
        pltpu.make_async_copy(forward_ref, forward_hbm.at[:, :, rows, :], sems.at[0]),
        pltpu.make_async_copy(backward_ref, backward_hbm.at[:, :, rows, :], sems.at[1]),
    ]
    for copy in copies:
        copy.start()
    for copy in copies:
        copy.wait()


VMEM = pl.BlockSpec(memory_space=pltpu.VMEM)
HBM = pl.BlockSpec(memory_space=pltpu.HBM)


def call(kernel, out_shapes, *operands, in_specs=None, out_specs=None, **kw):
    shapes = [jax.ShapeDtypeStruct(s, jnp.float32) for s in out_shapes]
    return pl.pallas_call(
        kernel,
        out_shape=shapes,
        in_specs=in_specs or [VMEM] * len(operands),
        out_specs=out_specs or [VMEM] * len(shapes),
        compiler_params=pltpu.CompilerParams(vmem_limit_bytes=LIMIT),
        **kw,
    )(*operands)


def local(rhs, coeffs, transmit, counts, elec_x, elec_y):
    slots, sources, height, width = rhs.shape
    devices = lax.axis_size("layer")
    levels = devices.bit_length() - 1
    half = height // 2
    message = (2 * sources + 2, half, width)

    def peer(place, bit):
        return place ^ bit ^ half_of(bit & -2)

    def exchange(x, *bits):
        pairs = [(i, peer(i, bits[half_of(i) % len(bits)])) for i in range(devices)]
        return lax.ppermute(x, "layer", pairs)

    keep, send, solved, factor, active = call(
        solve_kernel,
        [message, message, rhs.shape, transmit.shape, (slots, half, width)],
        *(pltpu.with_memory_space_constraint(a, pltpu.HBM) for a in (rhs, coeffs, transmit, counts, elec_x, elec_y)),
        in_specs=[HBM] * 6,
        scratch_shapes=[
            pltpu.VMEM(rhs.shape, jnp.float32),
            pltpu.VMEM(coeffs.shape, jnp.float32),
            pltpu.VMEM(transmit.shape, jnp.float32),
            pltpu.SMEM(counts.shape, jnp.int32),
            pltpu.SMEM(elec_x.shape, jnp.int32),
            pltpu.SMEM(elec_y.shape, jnp.int32),
            pltpu.VMEM((slots, sources, height + 2 * PAD, width), jnp.float32),
            pltpu.SemaphoreType.DMA((6,)),
        ],
    )
    top = levels - 1
    phases = [(0,)] + [
        tuple(range(first, min(first + WIDTH, top))) for first in range(1, top, WIDTH)
    ]
    walk, own, sent = [], keep, send
    for number, phase in enumerate(phases):
        maps = [own]
        count = (1 << len(phase)) - 1
        for index in range(count):
            other = TURN[index] if count == 3 else index
            maps.append(exchange(sent, (index + 1) << phase[0], (other + 1) << phase[0]))
        last = number == len(phases) - 1
        own, *extra = call(
            functools.partial(merge_kernel, phase, top if last else None),
            [message] + ([(sources + 1, half, width)] if last else []),
            *maps,
        )
        sent = own
        walk += maps
    got = exchange(extra[0], 1 << top)
    carry = (2 * sources, half, width)
    form, = call(
        functools.partial(prepare_kernel, phases, top),
        [(2, 3 * sources + 2, half, width)],
        *walk, own,
    )
    stay, passed = call(down_kernel, [carry, carry], form, got)
    came = exchange(passed, 1)

    def finish(offset, carried, *earlier):
        return call(
            functools.partial(finish_kernel, offset),
            [rhs.shape, rhs.shape],
            carried, solved, factor, active,
            *(pltpu.with_memory_space_constraint(e, pltpu.HBM) for e in earlier),
            in_specs=[VMEM] * 4 + [HBM] * len(earlier),
            out_specs=[HBM] * 2,
            scratch_shapes=[
                pltpu.VMEM((slots, sources, half, width), jnp.float32),
                pltpu.VMEM((slots, sources, half, width), jnp.float32),
                pltpu.SemaphoreType.DMA((2,)),
            ],
            input_output_aliases={4 + n: n for n in range(len(earlier))},
        )

    forward, backward = finish(1, came, *finish(0, stay))
    return forward, backward


def solution(mesh):
    placed = (
        P("layer", "grp", None, None),
        P("layer", None, None, None),
        P("layer", None, None),
        P(),
        P("grp"),
        P("grp"),
    )
    return jax.shard_map(
        local,
        mesh=mesh,
        in_specs=placed,
        out_specs=(P("layer", "grp", None, None), P("layer", "grp", None, None)),
        check_vma=False,
    )
```

```python
import functools

import jax
import jax.numpy as jnp
from jax import lax
from jax.experimental import pallas as pl
from jax.experimental.pallas import tpu as pltpu
from jax.sharding import PartitionSpec as P

CHEB = 4
HALF_WIDTH = 0.72
INJECTED = 4.0
OFFSETS = (
    (1, 0),
    (-1, 0),
    (0, 1),
    (0, -1),
    (2, 0),
    (-2, 0),
    (0, 2),
    (0, -2),
    (1, 1),
    (1, -1),
    (-1, 1),
    (-1, -1),
)
PAD = 8
LIMIT = 4 << 20
WIDTH = 2
FIRST = (1, 0, 2)
SECOND = (1, 2, 0)
CROSSED = (1, 2, 3)


def cheb_constants(passes):
    sigma = 1.0 / HALF_WIDTH
    rho_old = 1.0 / sigma
    out = []
    for _ in range(passes - 1):
        rho_new = 1.0 / (2.0 * sigma - rho_old)
        out.append((rho_new * rho_old, 2.0 * rho_new / HALF_WIDTH))
        rho_old = rho_new
    return out


def prepare_ratios(coeff, width):
    inverse = 1.0 / coeff[0]
    lane = lax.broadcasted_iota(jnp.int32, inverse.shape, 1)
    groups = {}
    for number, (step_x, step_y) in enumerate(OFFSETS):
        ratio = coeff[number + 1] * inverse
        if step_y:
            inside = (lane + step_y >= 0) & (lane + step_y < width)
            ratio = pltpu.roll(jnp.where(inside, ratio, 0.0), step_y % width, 1)
        groups.setdefault(step_y, []).append((step_x, ratio))
    return inverse, groups


def solve_kernel(
    rhs_hbm, coeff_hbm, transmit_hbm, counts_hbm, ex_hbm, ey_hbm,
    keep_ref, send_ref, solved_ref, factor_ref, active_ref,
    rhs_v, coeff_v, transmit_v, counts_s, ex_s, ey_s, field, sems,
):
    slots, sources, height, width = rhs_v.shape
    copies = [
        pltpu.make_async_copy(counts_hbm, counts_s, sems.at[0]),
        pltpu.make_async_copy(ex_hbm, ex_s, sems.at[1]),
        pltpu.make_async_copy(ey_hbm, ey_s, sems.at[2]),
        pltpu.make_async_copy(coeff_hbm, coeff_v, sems.at[3]),
        pltpu.make_async_copy(rhs_hbm, rhs_v, sems.at[4]),
        pltpu.make_async_copy(transmit_hbm, transmit_v, sems.at[5]),
    ]
    for copy in copies:
        copy.start()
    position = lax.axis_index("layer")
    zeros = jnp.zeros((PAD, width), jnp.float32)
    for slot in range(slots):
        for source in range(sources):
            field[slot, source, 0:PAD, :] = zeros
            field[slot, source, PAD + height : 2 * PAD + height, :] = zeros
    for copy in copies:
        copy.wait()

    row = lax.broadcasted_iota(jnp.int32, (height, width), 0)
    lane = lax.broadcasted_iota(jnp.int32, (height, width), 1)
    strength = jnp.where(position == 0, INJECTED, 0.0)
    constants = cheb_constants(CHEB)

    def stencil(slot, source, x, groups):
        field[slot, source, PAD : PAD + height, :] = x
        moved = {0: x}
        for step in (-2, -1, 1, 2):
            moved[step] = field[slot, source, PAD + step : PAD + step + height, :]
        total = None
        for step_y, members in groups.items():
            part = None
            for step_x, ratio in members:
                term = ratio * moved[step_x]
                part = term if part is None else part + term
            if step_y:
                part = pltpu.roll(part, (-step_y) % width, 1)
            total = part if total is None else total + part
        return total

    x, update, scaled, groups = {}, {}, {}, {}
    for slot in range(slots):
        inverse, groups[slot] = prepare_ratios(coeff_v[slot], width)
        for source in range(sources):
            forcing = rhs_v[slot, source]
            if slot == 0:
                at = (row == ex_s[source]) & (lane == ey_s[source])
                forcing = forcing + jnp.where(at, strength, 0.0)
            scaled[slot, source] = forcing * inverse
    x, update = dict(scaled), dict(scaled)
    for number, (momentum, weight) in enumerate(constants):
        for slot in range(slots):
            for source in range(sources):
                k = slot, source
                total = stencil(slot, source, x[k], groups[slot])
                update[k] = momentum * update[k] + weight * (scaled[k] - x[k] + total)
                x[k] = x[k] + update[k]
    for k in x:
        solved_ref[k[0], k[1]] = x[k]

    own_count = counts_s[position]
    factors = [transmit_v[slot] for slot in range(slots)]
    flags = [slot < own_count for slot in range(slots)]
    for slot in range(slots):
        factor_ref[slot] = factors[slot]
        active_ref[slot] = jnp.where(flags[slot], 1.0, jnp.zeros((height // 2, width), jnp.float32))
    scale = jnp.ones((height, width), jnp.float32)
    responses = []
    for slot in range(slots):
        scale = jnp.where(flags[slot], factors[slot] * scale, scale)
        responses.append(scale)
    bounce = jnp.zeros((height, width), jnp.float32)
    for slot in reversed(range(slots)):
        bounce = jnp.where(flags[slot], responses[slot] + factors[slot] * bounce, bounce)
    left_core = half_of(position) == 0

    def put(index, plane):
        top, bottom = plane[: height // 2], plane[height // 2 :]
        keep_ref[index] = jnp.where(left_core, top, bottom)
        send_ref[index] = jnp.where(left_core, bottom, top)

    put(2 * sources, scale)
    put(2 * sources + 1, bounce)
    for source in range(sources):
        down = jnp.zeros((height, width), jnp.float32)
        values = []
        for slot in range(slots):
            down = jnp.where(flags[slot], solved_ref[slot, source] + factors[slot] * down, down)
            values.append(down)
        up = jnp.zeros((height, width), jnp.float32)
        for slot in reversed(range(slots)):
            up = jnp.where(flags[slot], values[slot] + factors[slot] * up, up)
        put(source, down)
        put(sources + source, up)


def half_of(place):
    half = place & 1
    for level in CROSSED:
        half = half ^ ((place >> level) & 1)
    return half


def bit_of(level):
    return (lax.axis_index("layer") & (1 << level)) != 0


def in_order(items, bits):
    items = list(items)
    for number, bit in enumerate(bits):
        step = 1 << number
        items = [
            jnp.where(bit, items[index ^ step], items[index]) for index in range(len(items))
        ]
    return items


def planes(refs, index, bits):
    own, *others = [ref[index] for ref in refs]
    if len(others) == 3:
        second = half_of(lax.axis_index("layer")) == 1
        others = [jnp.where(second, others[SECOND.index(k)], others[FIRST.index(k)]) for k in range(3)]
    return in_order([own] + others, bits)


def merge_kernel(levels, top, *refs):
    count = 1 << len(levels)
    maps, out_ref = refs[:count], refs[count]
    sources = (out_ref.shape[0] - 2) // 2
    bits = [bit_of(level) for level in levels]
    scales = planes(maps, 2 * sources, bits)
    bounces = planes(maps, 2 * sources + 1, bits)
    scale, bounce = scales[0], bounces[0]
    before = [None]
    for place in range(1, count):
        before.append(scale)
        bounce = bounce + scale * scale * bounces[place]
        scale = scale * scales[place]
    out_ref[2 * sources] = scale
    out_ref[2 * sources + 1] = bounce
    if top is not None:
        right = bit_of(top)
        refs[count + 1][sources] = bounce
    for source in range(sources):
        downs = planes(maps, source, bits)
        ups = planes(maps, sources + source, bits)
        down, up = downs[0], ups[0]
        for place in range(1, count):
            up = up + before[place] * (ups[place] + bounces[place] * down)
            down = scales[place] * down + downs[place]
        out_ref[source] = down
        out_ref[sources + source] = up
        if top is not None:
            refs[count + 1][source] = jnp.where(right, up, down)


def prepare_kernel(phases, top, *refs):
    refs = list(refs)
    groups = [[refs.pop(0) for _ in range(1 << len(levels))] for levels in phases]
    whole_ref, out_ref = refs
    sources = (whole_ref.shape[0] - 2) // 2
    right = bit_of(top)

    def walk(source):
        if source is None:
            enter, back = (1.0,), (0.0, 1.0)
        else:
            enter, back = (0.0,), (0.0,)
        for number in reversed(range(len(phases))):
            maps, levels = groups[number], phases[number]
            bits = [bit_of(level) for level in levels]
            scales = planes(maps, 2 * sources, bits)
            bounces = planes(maps, 2 * sources + 1, bits)
            if source is not None:
                downs = planes(maps, source, bits)
                ups = planes(maps, sources + source, bits)
            enters, backs = [enter], [back]
            for place in range(len(maps) - 1):
                value = scales[place] * enters[-1][0]
                enters.append((value if source is None else value + downs[place],))
            for place in reversed(range(1, len(maps))):
                value = bounces[place] * enters[place][0] + scales[place] * backs[-1][0]
                if source is None:
                    backs.append((value, scales[place] * backs[-1][1]))
                else:
                    backs.append((ups[place] + value,))
            enters = list(zip(*(in_order(part, bits) for part in zip(*enters))))
            backs = list(zip(*(in_order(part, bits) for part in zip(*backs[::-1]))))
            enter, back = enters[0], backs[0]
        return enters[:2], backs[:2]

    enters, backs = walk(None)
    through = []
    for who in range(2):
        (alpha,), (delta, epsilon) = enters[who], backs[who]
        out_ref[who, 3 * sources] = jnp.where(right, alpha, 0.0)
        out_ref[who, 3 * sources + 1] = jnp.where(right, delta, epsilon)
        through.append(jnp.where(right, 0.0, epsilon))
    for source in range(sources):
        enters, backs = walk(source)
        for who in range(2):
            out_ref[who, source] = enters[who][0]
            out_ref[who, sources + source] = backs[who][0]
            out_ref[who, 2 * sources + source] = through[who] * whole_ref[source]


def down_kernel(form_ref, top_ref, stay_ref, pass_ref):
    sources = stay_ref.shape[0] // 2
    bounce = top_ref[sources]
    for who, out_ref in ((1, pass_ref), (0, stay_ref)):
        down, up = form_ref[who, 3 * sources], form_ref[who, 3 * sources + 1]
        for source in range(sources):
            got = top_ref[source]
            out_ref[source] = form_ref[who, source] + down * got
            out_ref[sources + source] = (
                form_ref[who, sources + source]
                + up * got
                + form_ref[who, 2 * sources + source] * bounce
            )


def finish_kernel(
    offset, carry_ref, solved_ref, transmit_ref, active_ref, *refs
):
    forward_hbm, backward_hbm, forward_ref, backward_ref, sems = refs[-5:]
    slots, sources, half, width = forward_ref.shape
    which = half_of(lax.axis_index("layer")) ^ offset
    rows = pl.ds(pl.multiple_of(which * half, half), half)
    flags = [active_ref[slot] > 0.0 for slot in range(slots)]
    factors = [transmit_ref[slot, rows, :] for slot in range(slots)]
    for source in range(sources):
        down, up = carry_ref[source], carry_ref[sources + source]
        values = []
        for slot in range(slots):
            value = solved_ref[slot, source, rows, :] + factors[slot] * down
            down = jnp.where(flags[slot], value, down)
            values.append(value)
            forward_ref[slot, source] = jnp.where(flags[slot], value, 0.0)
        for slot in reversed(range(slots)):
            value = values[slot] + factors[slot] * up
            up = jnp.where(flags[slot], value, up)
            backward_ref[slot, source] = jnp.where(flags[slot], value, 0.0)
    copies = [
        pltpu.make_async_copy(forward_ref, forward_hbm.at[:, :, rows, :], sems.at[0]),
        pltpu.make_async_copy(backward_ref, backward_hbm.at[:, :, rows, :], sems.at[1]),
    ]
    for copy in copies:
        copy.start()
    for copy in copies:
        copy.wait()


VMEM = pl.BlockSpec(memory_space=pltpu.VMEM)
HBM = pl.BlockSpec(memory_space=pltpu.HBM)


def call(kernel, out_shapes, *operands, in_specs=None, out_specs=None, **kw):
    shapes = [jax.ShapeDtypeStruct(s, jnp.float32) for s in out_shapes]
    return pl.pallas_call(
        kernel,
        out_shape=shapes,
        in_specs=in_specs or [VMEM] * len(operands),
        out_specs=out_specs or [VMEM] * len(shapes),
        compiler_params=pltpu.CompilerParams(vmem_limit_bytes=LIMIT),
        **kw,
    )(*operands)


def local(rhs, coeffs, transmit, counts, elec_x, elec_y):
    slots, sources, height, width = rhs.shape
    devices = lax.axis_size("layer")
    levels = devices.bit_length() - 1
    half = height // 2
    message = (2 * sources + 2, half, width)

    def peer(place, bit):
        return place ^ bit ^ half_of(bit & -2)

    def exchange(x, *bits):
        pairs = [(i, peer(i, bits[half_of(i) % len(bits)])) for i in range(devices)]
        return lax.ppermute(x, "layer", pairs)

    keep, send, solved, factor, active = call(
        solve_kernel,
        [message, message, rhs.shape, transmit.shape, (slots, half, width)],
        *(pltpu.with_memory_space_constraint(a, pltpu.HBM) for a in (rhs, coeffs, transmit, counts, elec_x, elec_y)),
        in_specs=[HBM] * 6,
        scratch_shapes=[
            pltpu.VMEM(rhs.shape, jnp.float32),
            pltpu.VMEM(coeffs.shape, jnp.float32),
            pltpu.VMEM(transmit.shape, jnp.float32),
            pltpu.SMEM(counts.shape, jnp.int32),
            pltpu.SMEM(elec_x.shape, jnp.int32),
            pltpu.SMEM(elec_y.shape, jnp.int32),
            pltpu.VMEM((slots, sources, height + 2 * PAD, width), jnp.float32),
            pltpu.SemaphoreType.DMA((6,)),
        ],
    )
    top = levels - 1
    phases = [(0,)] + [
        tuple(range(first, min(first + WIDTH, top))) for first in range(1, top, WIDTH)
    ]
    walk, own, sent = [], keep, send
    for number, phase in enumerate(phases):
        maps = [own]
        count = (1 << len(phase)) - 1
        for index in range(count):
            pair = (FIRST[index], SECOND[index]) if count == 3 else (index, index)
            maps.append(exchange(sent, *((k + 1) << phase[0] for k in pair)))
        last = number == len(phases) - 1
        own, *extra = call(
            functools.partial(merge_kernel, phase, top if last else None),
            [message] + ([(sources + 1, half, width)] if last else []),
            *maps,
        )
        sent = own
        walk += maps
    got = exchange(extra[0], 1 << top)
    carry = (2 * sources, half, width)
    form, = call(
        functools.partial(prepare_kernel, phases, top),
        [(2, 3 * sources + 2, half, width)],
        *walk, own,
    )
    stay, passed = call(down_kernel, [carry, carry], form, got)
    came = exchange(passed, 1)

    def finish(offset, carried, *earlier):
        return call(
            functools.partial(finish_kernel, offset),
            [rhs.shape, rhs.shape],
            carried, solved, factor, active,
            *(pltpu.with_memory_space_constraint(e, pltpu.HBM) for e in earlier),
            in_specs=[VMEM] * 4 + [HBM] * len(earlier),
            out_specs=[HBM] * 2,
            scratch_shapes=[
                pltpu.VMEM((slots, sources, half, width), jnp.float32),
                pltpu.VMEM((slots, sources, half, width), jnp.float32),
                pltpu.SemaphoreType.DMA((2,)),
            ],
            input_output_aliases={4 + n: n for n in range(len(earlier))},
        )

    forward, backward = finish(1, came, *finish(0, stay))
    return forward, backward


def solution(mesh):
    placed = (
        P("layer", "grp", None, None),
        P("layer", None, None, None),
        P("layer", None, None),
        P(),
        P("grp"),
        P("grp"),
    )
    return jax.shard_map(
        local,
        mesh=mesh,
        in_specs=placed,
        out_specs=(P("layer", "grp", None, None), P("layer", "grp", None, None)),
        check_vma=False,
    )
```

```python
import functools

import jax
import jax.numpy as jnp
from jax import lax
from jax.experimental import pallas as pl
from jax.experimental.pallas import tpu as pltpu
from jax.sharding import PartitionSpec as P

CHEB = 4
HALF_WIDTH = 0.72
INJECTED = 4.0
OFFSETS = (
    (1, 0),
    (-1, 0),
    (0, 1),
    (0, -1),
    (2, 0),
    (-2, 0),
    (0, 2),
    (0, -2),
    (1, 1),
    (1, -1),
    (-1, 1),
    (-1, -1),
)
PAD = 8
LIMIT = 4 << 20
WIDTH = 2
FIRST = (1, 0, 2)
SECOND = (1, 2, 0)
CROSSED = (1, 2, 3)


def cheb_constants(passes):
    sigma = 1.0 / HALF_WIDTH
    rho_old = 1.0 / sigma
    out = []
    for _ in range(passes - 1):
        rho_new = 1.0 / (2.0 * sigma - rho_old)
        out.append((rho_new * rho_old, 2.0 * rho_new / HALF_WIDTH))
        rho_old = rho_new
    return out


def prepare_ratios(coeff, width):
    inverse = 1.0 / coeff[0]
    lane = lax.broadcasted_iota(jnp.int32, inverse.shape, 1)
    groups = {}
    for number, (step_x, step_y) in enumerate(OFFSETS):
        ratio = coeff[number + 1] * inverse
        if step_y:
            inside = (lane + step_y >= 0) & (lane + step_y < width)
            ratio = pltpu.roll(jnp.where(inside, ratio, 0.0), step_y % width, 1)
        groups.setdefault(step_y, []).append((step_x, ratio))
    return inverse, groups


def solve_kernel(
    rhs_hbm, coeff_hbm, transmit_hbm, counts_hbm, ex_hbm, ey_hbm,
    keep_ref, send_ref, solved_ref, factor_ref, active_ref,
    rhs_v, coeff_v, transmit_v, counts_s, ex_s, ey_s, field, sems,
):
    slots, sources, height, width = rhs_v.shape
    copies = [
        pltpu.make_async_copy(counts_hbm, counts_s, sems.at[0]),
        pltpu.make_async_copy(ex_hbm, ex_s, sems.at[1]),
        pltpu.make_async_copy(ey_hbm, ey_s, sems.at[2]),
        pltpu.make_async_copy(coeff_hbm, coeff_v, sems.at[3]),
        pltpu.make_async_copy(rhs_hbm, rhs_v, sems.at[4]),
        pltpu.make_async_copy(transmit_hbm, transmit_v, sems.at[5]),
    ]
    for copy in copies:
        copy.start()
    position = lax.axis_index("layer")
    zeros = jnp.zeros((PAD, width), jnp.float32)
    for slot in range(slots):
        for source in range(sources):
            field[slot, source, 0:PAD, :] = zeros
            field[slot, source, PAD + height : 2 * PAD + height, :] = zeros
    for copy in copies:
        copy.wait()

    row = lax.broadcasted_iota(jnp.int32, (height, width), 0)
    lane = lax.broadcasted_iota(jnp.int32, (height, width), 1)
    strength = jnp.where(position == 0, INJECTED, 0.0)
    constants = cheb_constants(CHEB)

    def stencil(slot, source, x, groups):
        field[slot, source, PAD : PAD + height, :] = x
        moved = {0: x}
        for step in (-2, -1, 1, 2):
            moved[step] = field[slot, source, PAD + step : PAD + step + height, :]
        total = None
        for step_y, members in groups.items():
            part = None
            for step_x, ratio in members:
                term = ratio * moved[step_x]
                part = term if part is None else part + term
            if step_y:
                part = pltpu.roll(part, (-step_y) % width, 1)
            total = part if total is None else total + part
        return total

    x, update, scaled, groups = {}, {}, {}, {}
    for slot in range(slots):
        inverse, groups[slot] = prepare_ratios(coeff_v[slot], width)
        for source in range(sources):
            forcing = rhs_v[slot, source]
            if slot == 0:
                at = (row == ex_s[source]) & (lane == ey_s[source])
                forcing = forcing + jnp.where(at, strength, 0.0)
            scaled[slot, source] = forcing * inverse
    x, update = dict(scaled), dict(scaled)
    for number, (momentum, weight) in enumerate(constants):
        for slot in range(slots):
            for source in range(sources):
                k = slot, source
                total = stencil(slot, source, x[k], groups[slot])
                if number:
                    total = scaled[k] - x[k] + total
                update[k] = momentum * update[k] + weight * total
                x[k] = x[k] + update[k]
    for k in x:
        solved_ref[k[0], k[1]] = x[k]

    own_count = counts_s[position]
    factors = [transmit_v[slot] for slot in range(slots)]
    flags = [slot < own_count for slot in range(slots)]
    for slot in range(slots):
        factor_ref[slot] = factors[slot]
        active_ref[slot] = jnp.where(flags[slot], 1.0, jnp.zeros((height // 2, width), jnp.float32))
    scale = jnp.ones((height, width), jnp.float32)
    responses = []
    for slot in range(slots):
        scale = jnp.where(flags[slot], factors[slot] * scale, scale)
        responses.append(scale)
    bounce = jnp.zeros((height, width), jnp.float32)
    for slot in reversed(range(slots)):
        bounce = jnp.where(flags[slot], responses[slot] + factors[slot] * bounce, bounce)
    left_core = half_of(position) == 0

    def put(index, plane):
        top, bottom = plane[: height // 2], plane[height // 2 :]
        keep_ref[index] = jnp.where(left_core, top, bottom)
        send_ref[index] = jnp.where(left_core, bottom, top)

    put(2 * sources, scale)
    put(2 * sources + 1, bounce)
    for source in range(sources):
        down = jnp.zeros((height, width), jnp.float32)
        values = []
        for slot in range(slots):
            down = jnp.where(flags[slot], solved_ref[slot, source] + factors[slot] * down, down)
            values.append(down)
        up = jnp.zeros((height, width), jnp.float32)
        for slot in reversed(range(slots)):
            up = jnp.where(flags[slot], values[slot] + factors[slot] * up, up)
        put(source, down)
        put(sources + source, up)


def half_of(place):
    half = place & 1
    for level in CROSSED:
        half = half ^ ((place >> level) & 1)
    return half


def bit_of(level):
    return (lax.axis_index("layer") & (1 << level)) != 0


def in_order(items, bits):
    items = list(items)
    for number, bit in enumerate(bits):
        step = 1 << number
        items = [
            jnp.where(bit, items[index ^ step], items[index]) for index in range(len(items))
        ]
    return items


def planes(refs, index, bits):
    own, *others = [ref[index] for ref in refs]
    if len(others) == 3:
        second = half_of(lax.axis_index("layer")) == 1
        others = [jnp.where(second, others[SECOND.index(k)], others[FIRST.index(k)]) for k in range(3)]
    return in_order([own] + others, bits)


def merge_kernel(levels, top, *refs):
    count = 1 << len(levels)
    maps, out_ref = refs[:count], refs[count]
    sources = (out_ref.shape[0] - 2) // 2
    bits = [bit_of(level) for level in levels]
    scales = planes(maps, 2 * sources, bits)
    bounces = planes(maps, 2 * sources + 1, bits)
    scale, bounce = scales[0], bounces[0]
    before = [None]
    for place in range(1, count):
        before.append(scale)
        bounce = bounce + scale * scale * bounces[place]
        scale = scale * scales[place]
    out_ref[2 * sources] = scale
    out_ref[2 * sources + 1] = bounce
    if top is not None:
        right = bit_of(top)
        refs[count + 1][sources] = bounce
    for source in range(sources):
        downs = planes(maps, source, bits)
        ups = planes(maps, sources + source, bits)
        down, up = downs[0], ups[0]
        for place in range(1, count):
            up = up + before[place] * (ups[place] + bounces[place] * down)
            down = scales[place] * down + downs[place]
        out_ref[source] = down
        out_ref[sources + source] = up
        if top is not None:
            refs[count + 1][source] = jnp.where(right, up, down)


def prepare_kernel(phases, top, *refs):
    refs = list(refs)
    groups = [[refs.pop(0) for _ in range(1 << len(levels))] for levels in phases]
    whole_ref, out_ref = refs
    sources = (whole_ref.shape[0] - 2) // 2
    right = bit_of(top)

    def walk(source):
        if source is None:
            enter, back = (1.0,), (0.0, 1.0)
        else:
            enter, back = (0.0,), (0.0,)
        for number in reversed(range(len(phases))):
            maps, levels = groups[number], phases[number]
            bits = [bit_of(level) for level in levels]
            scales = planes(maps, 2 * sources, bits)
            bounces = planes(maps, 2 * sources + 1, bits)
            if source is not None:
                downs = planes(maps, source, bits)
                ups = planes(maps, sources + source, bits)
            enters, backs = [enter], [back]
            for place in range(len(maps) - 1):
                value = scales[place] * enters[-1][0]
                enters.append((value if source is None else value + downs[place],))
            for place in reversed(range(1, len(maps))):
                value = bounces[place] * enters[place][0] + scales[place] * backs[-1][0]
                if source is None:
                    backs.append((value, scales[place] * backs[-1][1]))
                else:
                    backs.append((ups[place] + value,))
            enters = list(zip(*(in_order(part, bits) for part in zip(*enters))))
            backs = list(zip(*(in_order(part, bits) for part in zip(*backs[::-1]))))
            enter, back = enters[0], backs[0]
        return enters[:2], backs[:2]

    enters, backs = walk(None)
    through = []
    for who in range(2):
        (alpha,), (delta, epsilon) = enters[who], backs[who]
        out_ref[who, 3 * sources] = jnp.where(right, alpha, 0.0)
        out_ref[who, 3 * sources + 1] = jnp.where(right, delta, epsilon)
        through.append(jnp.where(right, 0.0, epsilon))
    for source in range(sources):
        enters, backs = walk(source)
        for who in range(2):
            out_ref[who, source] = enters[who][0]
            out_ref[who, sources + source] = backs[who][0]
            out_ref[who, 2 * sources + source] = through[who] * whole_ref[source]


def down_kernel(form_ref, top_ref, stay_ref, pass_ref):
    sources = stay_ref.shape[0] // 2
    bounce = top_ref[sources]
    for who, out_ref in ((1, pass_ref), (0, stay_ref)):
        down, up = form_ref[who, 3 * sources], form_ref[who, 3 * sources + 1]
        for source in range(sources):
            got = top_ref[source]
            out_ref[source] = form_ref[who, source] + down * got
            out_ref[sources + source] = (
                form_ref[who, sources + source]
                + up * got
                + form_ref[who, 2 * sources + source] * bounce
            )


def finish_kernel(
    offset, carry_ref, solved_ref, transmit_ref, active_ref, *refs
):
    forward_hbm, backward_hbm, forward_ref, backward_ref, sems = refs[-5:]
    slots, sources, half, width = forward_ref.shape
    which = half_of(lax.axis_index("layer")) ^ offset
    rows = pl.ds(pl.multiple_of(which * half, half), half)
    flags = [active_ref[slot] > 0.0 for slot in range(slots)]
    factors = [transmit_ref[slot, rows, :] for slot in range(slots)]
    for source in range(sources):
        down, up = carry_ref[source], carry_ref[sources + source]
        values = []
        for slot in range(slots):
            value = solved_ref[slot, source, rows, :] + factors[slot] * down
            down = jnp.where(flags[slot], value, down)
            values.append(value)
            forward_ref[slot, source] = jnp.where(flags[slot], value, 0.0)
        for slot in reversed(range(slots)):
            value = values[slot] + factors[slot] * up
            up = jnp.where(flags[slot], value, up)
            backward_ref[slot, source] = jnp.where(flags[slot], value, 0.0)
    copies = [
        pltpu.make_async_copy(forward_ref, forward_hbm.at[:, :, rows, :], sems.at[0]),
        pltpu.make_async_copy(backward_ref, backward_hbm.at[:, :, rows, :], sems.at[1]),
    ]
    for copy in copies:
        copy.start()
    for copy in copies:
        copy.wait()


VMEM = pl.BlockSpec(memory_space=pltpu.VMEM)
HBM = pl.BlockSpec(memory_space=pltpu.HBM)


def call(kernel, out_shapes, *operands, in_specs=None, out_specs=None, **kw):
    shapes = [jax.ShapeDtypeStruct(s, jnp.float32) for s in out_shapes]
    return pl.pallas_call(
        kernel,
        out_shape=shapes,
        in_specs=in_specs or [VMEM] * len(operands),
        out_specs=out_specs or [VMEM] * len(shapes),
        compiler_params=pltpu.CompilerParams(vmem_limit_bytes=LIMIT),
        **kw,
    )(*operands)


def local(rhs, coeffs, transmit, counts, elec_x, elec_y):
    slots, sources, height, width = rhs.shape
    devices = lax.axis_size("layer")
    levels = devices.bit_length() - 1
    half = height // 2
    message = (2 * sources + 2, half, width)

    def peer(place, bit):
        return place ^ bit ^ half_of(bit & -2)

    def exchange(x, *bits):
        pairs = [(i, peer(i, bits[half_of(i) % len(bits)])) for i in range(devices)]
        return lax.ppermute(x, "layer", pairs)

    keep, send, solved, factor, active = call(
        solve_kernel,
        [message, message, rhs.shape, transmit.shape, (slots, half, width)],
        *(pltpu.with_memory_space_constraint(a, pltpu.HBM) for a in (rhs, coeffs, transmit, counts, elec_x, elec_y)),
        in_specs=[HBM] * 6,
        scratch_shapes=[
            pltpu.VMEM(rhs.shape, jnp.float32),
            pltpu.VMEM(coeffs.shape, jnp.float32),
            pltpu.VMEM(transmit.shape, jnp.float32),
            pltpu.SMEM(counts.shape, jnp.int32),
            pltpu.SMEM(elec_x.shape, jnp.int32),
            pltpu.SMEM(elec_y.shape, jnp.int32),
            pltpu.VMEM((slots, sources, height + 2 * PAD, width), jnp.float32),
            pltpu.SemaphoreType.DMA((6,)),
        ],
    )
    top = levels - 1
    phases = [(0,)] + [
        tuple(range(first, min(first + WIDTH, top))) for first in range(1, top, WIDTH)
    ]
    walk, own, sent = [], keep, send
    for number, phase in enumerate(phases):
        maps = [own]
        count = (1 << len(phase)) - 1
        for index in range(count):
            pair = (FIRST[index], SECOND[index]) if count == 3 else (index, index)
            maps.append(exchange(sent, *((k + 1) << phase[0] for k in pair)))
        last = number == len(phases) - 1
        own, *extra = call(
            functools.partial(merge_kernel, phase, top if last else None),
            [message] + ([(sources + 1, half, width)] if last else []),
            *maps,
        )
        sent = own
        walk += maps
    got = exchange(extra[0], 1 << top)
    carry = (2 * sources, half, width)
    form, = call(
        functools.partial(prepare_kernel, phases, top),
        [(2, 3 * sources + 2, half, width)],
        *walk, own,
    )
    stay, passed = call(down_kernel, [carry, carry], form, got)
    came = exchange(passed, 1)

    def finish(offset, carried, *earlier):
        return call(
            functools.partial(finish_kernel, offset),
            [rhs.shape, rhs.shape],
            carried, solved, factor, active,
            *(pltpu.with_memory_space_constraint(e, pltpu.HBM) for e in earlier),
            in_specs=[VMEM] * 4 + [HBM] * len(earlier),
            out_specs=[HBM] * 2,
            scratch_shapes=[
                pltpu.VMEM((slots, sources, half, width), jnp.float32),
                pltpu.VMEM((slots, sources, half, width), jnp.float32),
                pltpu.SemaphoreType.DMA((2,)),
            ],
            input_output_aliases={4 + n: n for n in range(len(earlier))},
        )

    forward, backward = finish(1, came, *finish(0, stay))
    return forward, backward


def solution(mesh):
    placed = (
        P("layer", "grp", None, None),
        P("layer", None, None, None),
        P("layer", None, None),
        P(),
        P("grp"),
        P("grp"),
    )
    return jax.shard_map(
        local,
        mesh=mesh,
        in_specs=placed,
        out_specs=(P("layer", "grp", None, None), P("layer", "grp", None, None)),
        check_vma=False,
    )
```
